512 devices in a mesh: ctx: 128 (over z, y_hi, x, core), tp: 4 (over y_lo).
Axes of the slice: x: 4, y: 8 (y_hi: 2, y_lo: 4; y = y_hi * 4 + y_lo), z: 8, core: 2. Of those that a mesh axis runs over, the one named last changes fastest.
Arguments:
- series: bfloat16 [131072, 1024], P(('ctx', 'tp'))
- w_query: bfloat16 [1024, 1024], P(None, 'tp')
- w_key: bfloat16 [1024, 1024], P(None, 'tp')
- w_value: bfloat16 [1024, 1024], P(None, 'tp'), may hold values from -0.1875 to 0.1875
- block_pos: int32 [128], replicated, may hold values from 0 to 127, as said below
Outputs:
- attended: bfloat16 [131072, 1024], P('ctx', 'tp')
The draws below stay inside these ranges and needn't reach their ends.
Inputs may be any that keep to these rules, and one draw needn't show every extreme that they name: Each block position appears exactly once, and block_pos[127] < block_pos[0].
All inputs are finite; a program needn't handle non-finite values.
Results may differ from the reference program's by a relative error of at most 0.0072.
Values may be sent and summed in bfloat16 or wider, within the bound.
No kernel may reach another device: no remote copies, remote signals or barrier semaphores. Data moves between devices by JAX's collectives and lax.ppermute only.
A program may use at most 64 MiB of HBM per device.

```python
import jax
import jax.numpy as jnp
from jax import lax

H = 8
HD = 128
D = 1024
BLOCK = 1024
SEQ = 131072
N_CTX = 128


def shared_weight(key):
    return jax.random.normal(key, (D, D), jnp.float32) * D ** (-0.5)


def draw_w_query(key, part):
    common = shared_weight(key)
    return common.astype(jnp.bfloat16)


def draw_w_key(key, part):
    key = jax.random.fold_in(key, 22)
    own_part = jax.random.normal(key, (D, D), jnp.float32) * D ** (-0.5)
    mixed = own_part
    return mixed.astype(jnp.bfloat16)


def draw_block_pos(key, part):
    key = jax.random.fold_in(key, 31)
    order = jax.random.permutation(key, N_CTX).astype(jnp.int32)
    first = order[0]
    final = order[N_CTX - 1]
    order = order.at[0].set(jnp.maximum(first, final))
    order = order.at[N_CTX - 1].set(jnp.minimum(first, final))
    return order.astype(jnp.int32)


def draw_series(key, part):
    key = jax.random.fold_in(key, 11)
    base_key = jax.random.fold_in(key, 0)
    base = jnp.clip(jax.random.normal(base_key, (SEQ, D), jnp.float32), -6.0, 6.0)
    return base.astype(jnp.bfloat16)


def level_of(own_key, shape, cuts, least, top_value):
    gain = 1.0
    for position, blocks in cuts:
        heights = jax.random.uniform(jax.random.fold_in(jax.random.fold_in(own_key, 6), position), (blocks,), jnp.float32, least / len(cuts), top_value / len(cuts))
        gain = gain * jnp.repeat(jnp.exp(heights), shape[position] // blocks).reshape((-1,) + (1,) * (len(shape) - 1 - position))
    return gain


def normal_values(key, extent, width, bound, pieces=(), dtype=jnp.bfloat16):
    level = level_of(key, extent, pieces, -0.22, 0.18) if pieces else 1.0
    array = jax.random.normal(key, extent, jnp.float32) * width * level
    return jnp.minimum(jnp.maximum(array, -bound), bound).astype(dtype)


def setup_inputs(seed: int = 0) -> dict:
    splits = jax.random.split(jax.random.key(seed), 6)
    series = draw_series(jax.random.fold_in(splits[5], 71), 0)
    w_query = draw_w_query(jax.random.fold_in(splits[5], 71), 0)
    w_key = draw_w_key(jax.random.fold_in(splits[5], 71), 0)
    w_value = normal_values(splits[3], (D, D), D ** -0.5, 0.1875, ((1, 4),))
    block_pos = draw_block_pos(jax.random.fold_in(splits[5], 71), 0)
    return dict(series=series, w_query=w_query, w_key=w_key, w_value=w_value, block_pos=block_pos)


def project_block(rows, w_query, w_key, w_value):
    query = jnp.dot(rows, w_query, preferred_element_type=jnp.float32).astype(jnp.bfloat16)
    key = jnp.dot(rows, w_key, preferred_element_type=jnp.float32).astype(jnp.bfloat16)
    value = jnp.dot(rows, w_value, preferred_element_type=jnp.float32).astype(jnp.bfloat16)
    return (query, key, value)

def attend_block(query, keys, values, allowed):
    count = query.shape[0]
    q_heads = query.reshape(count, H, HD).astype(jnp.float32)
    k_heads = keys.reshape(keys.shape[0], H, HD).astype(jnp.float32)
    v_heads = values.reshape(values.shape[0], H, HD).astype(jnp.float32)
    scores = jnp.einsum('qhd,khd->hqk', q_heads, k_heads) / jnp.sqrt(jnp.float32(HD))
    scores = jnp.where(allowed[None], scores, -jnp.inf)
    top = lax.optimization_barrier(jnp.max(scores, axis=-1, keepdims=True))
    weights = jnp.where(allowed[None], jnp.exp(scores - top), jnp.float32(0.0))
    total = lax.optimization_barrier(jnp.sum(weights, axis=-1))
    rounded = weights.astype(jnp.bfloat16).astype(jnp.float32)
    mixed = jnp.einsum('hqk,khd->qhd', rounded, v_heads) / jnp.transpose(total)[:, :, None]
    return mixed.reshape(count, H * HD).astype(jnp.bfloat16)

def reference(series, w_query, w_key, w_value, block_pos):
    last = lax.dynamic_slice_in_dim(series, (N_CTX - 1) * BLOCK, BLOCK, 0)
    first_q, first_k, first_v = project_block(last, w_query, w_key, w_value)
    rows = jnp.arange(BLOCK)
    causal = rows[None, :] <= rows[:, None]

    def step(carry, index):
        prev_k, prev_v = carry
        block = lax.dynamic_slice_in_dim(series, index * BLOCK, BLOCK, 0)
        query, key, value = project_block(block, w_query, w_key, w_value)
        prev_index = (index + N_CTX - 1) % N_CTX
        visible = block_pos[prev_index] < block_pos[index]
        allowed = jnp.concatenate([jnp.broadcast_to(visible, (BLOCK, BLOCK)), causal], axis=1)
        out = attend_block(query, jnp.concatenate([prev_k, key], 0), jnp.concatenate([prev_v, value], 0), allowed)
        return ((key, value), out)
    indices = jnp.arange(N_CTX).astype(jnp.int32)
    carry, outs = lax.scan(step, (first_k, first_v), indices)
    return outs.reshape(SEQ, D)
```

```python
import math

import jax
import jax.numpy as jnp
from jax import lax
from jax.experimental import pallas as pl
from jax.experimental.pallas import tpu as pltpu
from jax.sharding import PartitionSpec as P

HD = 128
HEADS = 2
WIDTH = HEADS * HD
CHUNK = 256
BLOCK = 4 * CHUNK
HEAD = 3 * CHUNK
DEPTH = 1024
SCALE = math.log2(math.e) / math.sqrt(HD)
ROW = 8

BF16 = jnp.bfloat16
F32 = jnp.float32
VMEM = pl.BlockSpec(memory_space=pltpu.VMEM)
SMEM = pl.BlockSpec(memory_space=pltpu.SMEM)
ANY = pl.BlockSpec(memory_space=pl.ANY)


def shape(rows, columns, dtype=BF16):
    return jax.ShapeDtypeStruct((rows, columns), dtype)


STATE = (shape(8, BLOCK, F32), shape(WIDTH, BLOCK, F32))


def run(body, out, specs, flops, *args, alias=None, scratch=()):
    return pl.pallas_call(
        body,
        out_shape=out,
        in_specs=specs,
        out_specs=jax.tree.map(lambda _: VMEM, out),
        scratch_shapes=list(scratch),
        input_output_aliases=alias or {},
        compiler_params=pltpu.CompilerParams(vmem_limit_bytes=20 << 20),
        cost_estimate=pl.CostEstimate(flops=flops, bytes_accessed=1 << 20, transcendentals=0),
    )(*args)


def dot(a, b, dims):
    return lax.dot_general(a, b, (dims, ((), ())), preferred_element_type=F32)


def project(rows, weight):
    return jnp.dot(rows, weight, preferred_element_type=F32).astype(BF16)


def head(number):
    return slice(number * HD, (number + 1) * HD)


def scores(keys, query):
    return dot(keys, query, ((1,), (1,))) * SCALE


def mixed(values, weights):
    return dot(values, weights.astype(BF16), ((0,), (0,)))


def positions(tp, chunks, axis):
    parts = []
    for chunk in chunks:
        size = (CHUNK, 1) if axis == 0 else (1, CHUNK)
        parts.append(lax.broadcasted_iota(jnp.int32, size, axis) + (tp ^ chunk) * CHUNK)
    return jnp.concatenate(parts, axis)


def first(found, values):
    top = jnp.max(found, axis=0, keepdims=True)
    weights = jnp.exp2(found - top)
    return top, jnp.sum(weights, axis=0, keepdims=True), mixed(values, weights)


def further(top0, total0, mix0, found, values):
    top = jnp.maximum(top0, jnp.max(found, axis=0, keepdims=True))
    weights = jnp.exp2(found - top)
    fade = jnp.exp2(top0 - top)
    total = total0 * fade + jnp.sum(weights, axis=0, keepdims=True)
    return top, total, mix0 * fade + mixed(values, weights)


def project_own_body(x, wq, wk, wv, q, kv):
    q[...] = project(x[...], wq[...])
    kv[:, :WIDTH] = project(x[...], wk[...])
    kv[:, WIDTH:] = project(x[...], wv[...])


def project_middle_body(xb, xc, qa, kva, wq, wk, wv, q, kv):
    q[:CHUNK] = qa[...]
    kv[:CHUNK] = kva[...]
    for place, x in ((1, xb), (2, xc)):
        rows = slice(place * CHUNK, (place + 1) * CHUNK)
        q[rows] = project(x[...], wq[...])
        kv[rows, :WIDTH] = project(x[...], wk[...])
        kv[rows, WIDTH:] = project(x[...], wv[...])


def project_last_body(info, outer, inner, wq, wk, wv, q, kv):
    middle = jnp.logical_or(info[0] == 1, info[0] == 2)
    x = jnp.where(middle, inner[...], outer[...])
    q[...] = project(x, wq[...])
    kv[:, :WIDTH] = project(x, wk[...])
    kv[:, WIDTH:] = project(x, wv[...])


def project_far_body(info, kva, xb, xc, xd, wk, wv, kv, x, w, sems):
    @pl.when(info[2] == 1)
    def _():
        copies = [pltpu.make_async_copy(source, x.at[n], sems.at[n]) for n, source in enumerate((xb, xc, xd))]
        copies += [pltpu.make_async_copy(source, w.at[n], sems.at[3 + n]) for n, source in enumerate((wk, wv))]
        copies.append(pltpu.make_async_copy(kva, kv.at[:CHUNK], sems.at[5]))
        for copy in copies:
            copy.start()
        for copy in copies:
            copy.wait()
        for n in range(3):
            rows = slice((n + 1) * CHUNK, (n + 2) * CHUNK)
            kv[rows, :WIDTH] = project(x[n], w[0])
            kv[rows, WIDTH:] = project(x[n], w[1])


def own_first_body(info, q, kv, state, mix):
    seen = positions(info[0], range(3), 0) <= positions(info[0], range(3), 1)
    for h in range(HEADS):
        found = jnp.where(seen, scores(kv[:, head(h)], q[:, head(h)]), -jnp.inf)
        top, total, part = first(found, kv[:, head(HEADS + h)])
        state[h : h + 1, :HEAD] = top
        state[HEADS + h : HEADS + h + 1, :HEAD] = total
        mix[head(h), :HEAD] = part


def before_first_body(info, q, near, far, state0, mix0, state, mix):
    @pl.when(info[1] == 1)
    def _():
        for h in range(HEADS):
            keys = jnp.where(info[2] == 1, far[:HEAD, head(h)], near[:, head(h)])
            values = jnp.where(info[2] == 1, far[:HEAD, head(HEADS + h)], near[:, head(HEADS + h)])
            top, total, part = further(
                state0[h : h + 1, :HEAD],
                state0[HEADS + h : HEADS + h + 1, :HEAD],
                mix0[head(h), :HEAD],
                scores(keys, q[:, head(h)]),
                values,
            )
            state[h : h + 1, :HEAD] = top
            state[HEADS + h : HEADS + h + 1, :HEAD] = total
            mix[head(h), :HEAD] = part

    @pl.when(info[1] == 0)
    def _():
        state[...] = state0[...]
        mix[...] = mix0[...]


def own_last_body(info, q, qd, kv, kvd, near, far, state0, mix0, state, mix):
    tp = info[0]
    seen = jnp.concatenate(
        [
            positions(tp, range(4), 0) <= positions(tp, (3,), 1),
            jnp.broadcast_to(info[1] == 1, (HEAD, CHUNK)),
        ],
        0,
    )
    seen_last = positions(tp, (3,), 0) <= positions(tp, range(3), 1)
    for h in range(HEADS):
        v = head(HEADS + h)
        keys = jnp.where(info[2] == 1, far[:HEAD, head(h)], near[:, head(h)])
        values = jnp.where(info[2] == 1, far[:HEAD, v], near[:, v])
        keys = jnp.concatenate([kv[:, head(h)], kvd[:, head(h)], keys], 0)
        values = jnp.concatenate([kv[:, v], kvd[:, v], values], 0)
        found = jnp.where(seen, scores(keys, qd[:, head(h)]), -jnp.inf)
        top, total, part = first(found, values)
        state[h : h + 1, HEAD:] = top
        state[HEADS + h : HEADS + h + 1, HEAD:] = total
        mix[head(h), HEAD:] = part
        top, total, part = further(
            state0[h : h + 1, :HEAD],
            state0[HEADS + h : HEADS + h + 1, :HEAD],
            mix0[head(h), :HEAD],
            jnp.where(seen_last, scores(kvd[:, head(h)], q[:, head(h)]), -jnp.inf),
            kvd[:, v],
        )
        state[h : h + 1, :HEAD] = top
        state[HEADS + h : HEADS + h + 1, :HEAD] = total
        mix[head(h), :HEAD] = part


def before_last_body(info, q, qd, near, far, state, mix, out):
    def store(h, total, part):
        part = (part / total).astype(BF16)
        for chunk in range(4):
            rows = pl.ds(pl.multiple_of((info[0] ^ chunk) * CHUNK, CHUNK), CHUNK)
            out[rows, head(h)] = part[:, chunk * CHUNK : (chunk + 1) * CHUNK].T

    for h in range(HEADS):
        total0 = state[HEADS + h : HEADS + h + 1, :]

        @pl.when(info[1] == 1)
        def _():
            v = head(HEADS + h)
            keys = jnp.where(info[2] == 1, far[HEAD:, head(h)], near[:, head(h)])
            values = jnp.where(info[2] == 1, far[HEAD:, v], near[:, v])
            query = jnp.concatenate([q[:, head(h)], qd[:, head(h)]], 0)
            _, total, part = further(state[h : h + 1, :], total0, mix[head(h), :], scores(keys, query), values)
            store(h, total, part)

        @pl.when(info[1] == 0)
        def _():
            store(h, total0, mix[head(h), :])


PAIR = 2 * 2 * HEADS * CHUNK * CHUNK * HD
TP = 4


def device(ctx, tp):
    return ctx * TP + tp


def line_ends(ctx_count):
    return [(i, (i + ctx_count - 1) % ctx_count) for i in range(0, ctx_count, ROW)]


def body(series, w_query, w_key, w_value, block_pos):
    ctx_count = lax.axis_size("ctx")
    here = lax.axis_index("ctx")
    tp = lax.axis_index("tp")
    before = (here + ctx_count - 1) % ctx_count
    visible = block_pos[before] < block_pos[here]
    far_here = here % ROW == 0
    info = jnp.stack([tp, visible.astype(jnp.int32), far_here.astype(jnp.int32)]).astype(jnp.int32)
    weights = (w_query, w_key, w_value)
    ends = line_ends(ctx_count)

    def swap(x, pairs):
        return lax.ppermute(x, "tp", pairs)

    def to_next(x):
        return lax.ppermute(x, "ctx", [(i - 1, i) for i in range(ctx_count) if i % ROW])

    def send(x, route):
        return lax.ppermute(x, ("ctx", "tp"), route)

    def aside(x, line, shards=range(TP), stay=()):
        route = [(device(last, t), device(last - ROW + 1 + line, t)) for _, last in ends for t in shards]
        return send(x, route + [(device(last, t), device(last, t)) for _, last in ends for t in stay])

    def across(x, chunk, line):
        return send(
            x,
            [(device(last - ROW + 1 + line(t ^ chunk), t ^ chunk), device(i, t)) for i, last in ends for t in range(TP)],
        )

    qa, kva = run(
        project_own_body,
        (shape(CHUNK, WIDTH), shape(CHUNK, 2 * WIDTH)),
        [VMEM] * 4,
        2 * CHUNK * DEPTH * 3 * WIDTH,
        series,
        *weights,
    )
    far_c = aside(series, 5)
    far_b = aside(series, 1, (1, 2), (0, 3))
    far_a = aside(kva, 3)
    xc = swap(series, [(t, t ^ 2) for t in range(TP)])
    xb = swap(series, [(t, t ^ 1) for t in range(TP)])
    far_d = across(series, 3, lambda t: 7)
    far_c = across(far_c, 2, lambda t: 5)
    far_b = across(far_b, 1, lambda t: 1 if t in (1, 2) else 7)
    far_a = across(far_a, 0, lambda t: 3)
    xc, xb, own = lax.optimization_barrier((xc, xb, series))
    outer = swap(xc, [(2, 3), (1, 0)])
    inner = swap(own, [(1, 2), (2, 1)])
    q, kv = run(
        project_middle_body,
        (shape(HEAD, WIDTH), shape(HEAD, 2 * WIDTH)),
        [VMEM] * 7,
        4 * CHUNK * DEPTH * 3 * WIDTH,
        xb,
        xc,
        qa,
        kva,
        *weights,
    )
    near = to_next(kv)
    state, mix = run(own_first_body, STATE, [SMEM] + [VMEM] * 2, 9 * PAIR, info, q, kv)
    kv_far = run(
        project_far_body,
        shape(BLOCK, 2 * WIDTH),
        [SMEM] + [ANY] * 6,
        8 * CHUNK * DEPTH * 2 * WIDTH,
        info,
        far_a,
        far_b,
        far_c,
        far_d,
        w_key,
        w_value,
        scratch=(
            pltpu.VMEM((3, CHUNK, DEPTH), BF16),
            pltpu.VMEM((2, DEPTH, WIDTH), BF16),
            pltpu.SemaphoreType.DMA((6,)),
        ),
    )
    outer, inner, kv_far = lax.optimization_barrier((outer, inner, kv_far))
    qd, kvd = run(
        project_last_body,
        (shape(CHUNK, WIDTH), shape(CHUNK, 2 * WIDTH)),
        [SMEM] + [VMEM] * 5,
        2 * CHUNK * DEPTH * 3 * WIDTH,
        info,
        outer,
        inner,
        *weights,
    )
    near_last = to_next(kvd)
    near, qd = lax.optimization_barrier((near, qd))
    state, mix = run(
        before_first_body,
        STATE,
        [SMEM] + [VMEM] * 5,
        9 * PAIR,
        info,
        q,
        near,
        kv_far,
        state,
        mix,
        alias={4: 0, 5: 1},
    )
    state, mix = run(
        own_last_body,
        STATE,
        [SMEM] + [VMEM] * 8,
        10 * PAIR,
        info,
        q,
        qd,
        kv,
        kvd,
        near,
        kv_far,
        state,
        mix,
        alias={7: 0, 8: 1},
    )
    return run(
        before_last_body,
        shape(BLOCK, WIDTH),
        [SMEM] + [VMEM] * 6,
        4 * PAIR,
        info,
        q,
        qd,
        near_last,
        kv_far,
        state,
        mix,
    )


def solution(mesh):
    in_specs = (P(("ctx", "tp"), None), P(None, "tp"), P(None, "tp"), P(None, "tp"), P())
    out_specs = P("ctx", "tp")
    return jax.shard_map(body, mesh=mesh, in_specs=in_specs, out_specs=out_specs, check_vma=False)
```

```python
import math

import jax
import jax.numpy as jnp
from jax import lax
from jax.experimental import pallas as pl
from jax.experimental.pallas import tpu as pltpu
from jax.sharding import PartitionSpec as P

HD = 128
HEADS = 2
WIDTH = HEADS * HD
CHUNK = 256
BLOCK = 4 * CHUNK
HEAD = 3 * CHUNK
DEPTH = 1024
SCALE = math.log2(math.e) / math.sqrt(HD)
ROW = 8
LAST = ROW - 1
LEAVE = (None, (3, 1, 1, 3), (5,) * 4, (LAST, 3, 3, LAST))

BF16 = jnp.bfloat16
F32 = jnp.float32
VMEM = pl.BlockSpec(memory_space=pltpu.VMEM)
SMEM = pl.BlockSpec(memory_space=pltpu.SMEM)
ANY = pl.BlockSpec(memory_space=pl.ANY)


def shape(rows, columns, dtype=BF16):
    return jax.ShapeDtypeStruct((rows, columns), dtype)


STATE = (shape(8, BLOCK, F32), shape(WIDTH, BLOCK, F32))


def run(name, body, out, specs, flops, *args, alias=None, scratch=(), out_specs=None):
    call = pl.pallas_call(
        body,
        out_shape=out,
        in_specs=specs,
        out_specs=out_specs or jax.tree.map(lambda _: VMEM, out),
        scratch_shapes=list(scratch),
        input_output_aliases=alias or {},
        compiler_params=pltpu.CompilerParams(vmem_limit_bytes=20 << 20),
        cost_estimate=pl.CostEstimate(flops=flops, bytes_accessed=0, transcendentals=0),
    )
    with jax.named_scope("n_" + name):
        return call(*args)


def dot(a, b, dims):
    return lax.dot_general(a, b, (dims, ((), ())), preferred_element_type=F32)


def project(rows, weight):
    return jnp.dot(rows, weight, preferred_element_type=F32).astype(BF16)


def head(number):
    return slice(number * HD, (number + 1) * HD)


def scores(keys, query):
    return dot(keys, query, ((1,), (1,))) * SCALE


def mixed(values, weights):
    return dot(values, weights.astype(BF16), ((0,), (0,)))


def positions(tp, chunks, axis):
    parts = []
    for chunk in chunks:
        size = (CHUNK, 1) if axis == 0 else (1, CHUNK)
        parts.append(lax.broadcasted_iota(jnp.int32, size, axis) + (tp ^ chunk) * CHUNK)
    return jnp.concatenate(parts, axis)


def first(found, values):
    top = jnp.max(found, axis=0, keepdims=True)
    weights = jnp.exp2(found - top)
    return top, jnp.sum(weights, axis=0, keepdims=True), mixed(values, weights)


def further(top0, total0, mix0, found, values):
    top = jnp.maximum(top0, jnp.max(found, axis=0, keepdims=True))
    weights = jnp.exp2(found - top)
    fade = jnp.exp2(top0 - top)
    total = total0 * fade + jnp.sum(weights, axis=0, keepdims=True)
    return top, total, mix0 * fade + mixed(values, weights)


def project_own_body(info, x, wq, wk, wv, q, kv):
    q[...] = project(x[...], wq[...])
    kv[:, :WIDTH] = project(x[...], wk[...])
    kv[:, WIDTH:] = project(x[...], wv[...])


def project_middle_body(xb, xc, qa, kva, wq, wk, wv, q, kv):
    q[:CHUNK] = qa[...]
    kv[:CHUNK] = kva[...]
    for place, x in ((1, xb), (2, xc)):
        rows = slice(place * CHUNK, (place + 1) * CHUNK)
        q[rows] = project(x[...], wq[...])
        kv[rows, :WIDTH] = project(x[...], wk[...])
        kv[rows, WIDTH:] = project(x[...], wv[...])


def project_last_body(info, outer, inner, wq, wk, wv, q, kv):
    middle = jnp.logical_or(info[0] == 1, info[0] == 2)
    x = jnp.where(middle, inner[...], outer[...])
    q[...] = project(x, wq[...])
    kv[:, :WIDTH] = project(x, wk[...])
    kv[:, WIDTH:] = project(x, wv[...])


def project_far_body(info, kva, xb, xc, xd, wk, wv, kv, kvd, x, w, sems):
    @pl.when(info[2] == 1)
    def _():
        copies = [pltpu.make_async_copy(source, x.at[n], sems.at[n]) for n, source in enumerate((xb, xc, xd))]
        copies += [pltpu.make_async_copy(source, w.at[n], sems.at[3 + n]) for n, source in enumerate((wk, wv))]
        copies.append(pltpu.make_async_copy(kva, kv.at[:CHUNK], sems.at[5]))
        for copy in copies:
            copy.start()
        for copy in copies:
            copy.wait()
        for n in range(3):
            out, rows = (kv, slice((n + 1) * CHUNK, (n + 2) * CHUNK)) if n < 2 else (kvd, slice(0, CHUNK))
            out[rows, :WIDTH] = project(x[n], w[0])
            out[rows, WIDTH:] = project(x[n], w[1])


def own_first_body(info, q, kv, state, mix):
    seen = positions(info[0], range(3), 0) <= positions(info[0], range(3), 1)
    for h in range(HEADS):
        found = jnp.where(seen, scores(kv[:, head(h)], q[:, head(h)]), -jnp.inf)
        top, total, part = first(found, kv[:, head(HEADS + h)])
        state[h : h + 1, :HEAD] = top
        state[HEADS + h : HEADS + h + 1, :HEAD] = total
        mix[head(h), :HEAD] = part


def pieces(units, states):
    found = []
    for query, parts in units:
        found.append([scores(keys, query) if seen is None else jnp.where(seen, scores(keys, query), -jnp.inf) for keys, _, seen in parts])
    ready = []
    for number, tiles in enumerate(found):
        top = tiles[0].max(axis=0, keepdims=True)
        for tile in tiles[1:]:
            top = jnp.maximum(top, tile.max(axis=0, keepdims=True))
        if states[number] is not None:
            top = jnp.maximum(top, states[number][0])
        weights = [jnp.exp2(tile - top) for tile in tiles]
        total = sum(w.sum(axis=0, keepdims=True) for w in weights)
        ready.append((top, total, [w.astype(BF16) for w in weights]))
    results = []
    for number, (top, total, weights) in enumerate(ready):
        part = sum(
            dot(values, w, ((0,), (0,))) for (_, values, _), w in zip(units[number][1], weights, strict=True)
        )
        if states[number] is not None:
            top0, total0, mix0 = states[number]
            fade = jnp.exp2(top0 - top)
            total = total + total0 * fade
            part = part + mix0 * fade
        results.append((top, total, part))
    return results


def middle_body(info, q, qd, kv, kvd, near, far, state0, mix0, state, mix):
    tp = info[0]
    last = tp ^ 3
    diagonal = positions(tp, (3,), 0) <= positions(tp, (3,), 1)

    def work(visible):
        for h in range(HEADS):
            k, v = head(h), head(HEADS + h)
            s, l = slice(h, h + 1), slice(HEADS + h, HEADS + h + 1)
            units, states, columns = [], [], []
            before = tuple(jnp.where(info[2] == 1, far[:, p], near[:, p]) for p in (k, v)) if visible else ()
            for chunk in range(4):
                rows = slice(chunk * CHUNK, (chunk + 1) * CHUNK)
                columns.append(rows)
                if chunk < 3:
                    parts = [(kvd[:, k], kvd[:, v], last < (tp ^ chunk))]
                    states.append((state0[s, rows], state0[l, rows], mix0[k, rows]))
                else:
                    parts = [(kvd[:, k], kvd[:, v], diagonal)]
                    for other in range(3):
                        these = slice(other * CHUNK, (other + 1) * CHUNK)
                        parts.append((kv[these, k], kv[these, v], (tp ^ other) < last))
                    states.append(None)
                if visible:
                    parts.append((*before, None))
                units.append((q[rows, k] if chunk < 3 else qd[:, k], parts))
            for rows, (top, total, part) in zip(columns, pieces(units, states), strict=True):
                state[s, rows] = top
                state[l, rows] = total
                mix[k, rows] = part

    @pl.when(info[1] == 1)
    def _():
        work(True)

    @pl.when(info[1] == 0)
    def _():
        work(False)


def last_body(info, q, qd, near, far, state, mix, out, held, done, sems):
    def finish(chunk, results):
        for h, (total, part) in enumerate(results):
            held[chunk, :, head(h)] = (part / total).astype(BF16).T
        rows = pl.ds(pl.multiple_of((info[0] ^ chunk) * CHUNK, CHUNK), CHUNK)
        pltpu.make_async_copy(held.at[chunk], out.at[rows], sems.at[chunk]).start()

    @pl.when(info[2] == 1)
    def _():
        copy = pltpu.make_async_copy(far, done, sems.at[4])
        copy.start()
        copy.wait()

    @pl.when(info[2] == 0)
    def _():
        done[...] = near[...]

    @pl.when(info[1] == 1)
    def _():
        for chunk in range(4):
            rows = slice(chunk * CHUNK, (chunk + 1) * CHUNK)
            units, states = [], []
            for h in range(HEADS):
                k, v = head(h), head(HEADS + h)
                units.append((q[rows, k] if chunk < 3 else qd[:, k], [(done[:, k], done[:, v], None)]))
                states.append((state[h : h + 1, rows], state[HEADS + h : HEADS + h + 1, rows], mix[k, rows]))
            finish(chunk, [(total, part) for _, total, part in pieces(units, states)])

    @pl.when(info[1] == 0)
    def _():
        for chunk in range(4):
            rows = slice(chunk * CHUNK, (chunk + 1) * CHUNK)
            finish(chunk, [(state[HEADS + h : HEADS + h + 1, rows], mix[head(h), rows]) for h in range(HEADS)])

    for chunk in range(4):
        rows = pl.ds(pl.multiple_of((info[0] ^ chunk) * CHUNK, CHUNK), CHUNK)
        pltpu.make_async_copy(held.at[chunk], out.at[rows], sems.at[chunk]).wait()


EARLY = 20_000_000_000
FAR = 4_000_000_000
TP = 4


def device(ctx, tp):
    return ctx * TP + tp


def line_ends(ctx_count):
    return [(i, (i + ctx_count - 1) % ctx_count) for i in range(0, ctx_count, ROW)]


def body(series, w_query, w_key, w_value, block_pos):
    ctx_count = lax.axis_size("ctx")
    here = lax.axis_index("ctx")
    tp = lax.axis_index("tp")
    before = (here + ctx_count - 1) % ctx_count
    visible = block_pos[before] < block_pos[here]
    far_here = here % ROW == 0
    info = jnp.stack([tp, visible.astype(jnp.int32), far_here.astype(jnp.int32)]).astype(jnp.int32)
    weights = (w_query, w_key, w_value)
    ends = line_ends(ctx_count)

    def send(name, x, route):
        with jax.named_scope("n_" + name):
            return lax.ppermute(x, ("ctx", "tp"), route)

    def swap(name, x, pairs):
        return send(name, x, [(device(i, a), device(i, b)) for i in range(ctx_count) for a, b in pairs])

    def to_next(name, x):
        return send(name, x, [(device(i - 1, t), device(i, t)) for i in range(ctx_count) if i % ROW for t in range(TP)])

    def place(last, first, line):
        return first // (2 * ROW) * (2 * ROW) + last % (2 * ROW) - LAST + line

    def aside(name, x, places):
        return send(name, x, [(device(last, t), device(place(last, i, places[t]), t)) for i, last in ends for t in range(TP)])

    def across(name, x, chunk, places=None):
        route = []
        for i, last in ends:
            for t in range(TP):
                shard = t ^ chunk
                source = last if places is None else place(last, i, places[shard])
                route.append((device(source, shard), device(i, t)))
        return send(name, x, route)

    xc = swap("xc", series, [(t, t ^ 2) for t in range(TP)])
    xb = swap("xb", series, [(t, t ^ 1) for t in range(TP)])
    qa, kva = run(
        "own",
        project_own_body,
        (shape(CHUNK, WIDTH), shape(CHUNK, 2 * WIDTH)),
        [SMEM] + [VMEM] * 4,
        0,
        info,
        series,
        *weights,
    )
    far_b, far_c, far_d = (aside(f"aside{chunk}", series, LEAVE[chunk]) for chunk in (1, 2, 3))
    xc, xb, own, qa, kva = lax.optimization_barrier((xc, xb, series, qa, kva))
    outer = swap("outer", xc, [(2, 3), (1, 0)])
    far_a, far_b, far_c, far_d = (
        across(f"across{chunk}", x, chunk, LEAVE[chunk]) for chunk, x in enumerate((kva, far_b, far_c, far_d))
    )
    own, far_d = lax.optimization_barrier((own, far_d))
    inner = swap("inner", own, [(1, 2), (2, 1)])
    q, kv = run(
        "middle",
        project_middle_body,
        (shape(HEAD, WIDTH), shape(HEAD, 2 * WIDTH)),
        [VMEM] * 7,
        0,
        xb,
        xc,
        qa,
        kva,
        *weights,
    )
    kv, far_c = lax.optimization_barrier((kv, far_c))
    near = to_next("near", kv)
    state, mix = run(
        "attend_own",
        own_first_body, STATE, [SMEM] + [VMEM] * 2, 0, info, q, kv)
    mix, far_a, far_b, far_c, far_d = lax.optimization_barrier((mix, far_a, far_b, far_c, far_d))
    far, far_last = run(
        "far",
        project_far_body,
        (shape(HEAD, 2 * WIDTH), shape(CHUNK, 2 * WIDTH)),
        [SMEM] + [ANY] * 6,
        FAR,
        info,
        far_a,
        far_b,
        far_c,
        far_d,
        w_key,
        w_value,
        scratch=(
            pltpu.VMEM((3, CHUNK, DEPTH), BF16),
            pltpu.VMEM((2, DEPTH, WIDTH), BF16),
            pltpu.SemaphoreType.DMA((6,)),
        ),
    )
    outer, inner, mix, far = lax.optimization_barrier((outer, inner, mix, far))
    qd, kvd = run(
        "last",
        project_last_body,
        (shape(CHUNK, WIDTH), shape(CHUNK, 2 * WIDTH)),
        [SMEM] + [VMEM] * 5,
        EARLY,
        info,
        outer,
        inner,
        *weights,
    )
    near_last = to_next("near_last", kvd)
    near, qd = lax.optimization_barrier((near, qd))
    state, mix = run(
        "attend_most",
        middle_body,
        STATE,
        [SMEM] + [VMEM] * 8,
        0,
        info,
        q,
        qd,
        kv,
        kvd,
        near,
        far,
        state,
        mix,
        alias={7: 0, 8: 1},
    )
    return run(
        "attend_last",
        last_body,
        shape(BLOCK, WIDTH),
        [SMEM] + [VMEM] * 3 + [ANY] + [VMEM] * 2,
        0,
        info,
        q,
        qd,
        near_last,
        far_last,
        state,
        mix,
        out_specs=ANY,
        scratch=(
            pltpu.VMEM((4, CHUNK, WIDTH), BF16),
            pltpu.VMEM((CHUNK, 2 * WIDTH), BF16),
            pltpu.SemaphoreType.DMA((5,)),
        ),
    )


def solution(mesh):
    in_specs = (P(("ctx", "tp"), None), P(None, "tp"), P(None, "tp"), P(None, "tp"), P())
    out_specs = P("ctx", "tp")
    return jax.shard_map(body, mesh=mesh, in_specs=in_specs, out_specs=out_specs, check_vma=False)
```

```python
import math

import jax
import jax.numpy as jnp
from jax import lax
from jax.experimental import pallas as pl
from jax.experimental.pallas import tpu as pltpu
from jax.sharding import PartitionSpec as P

HD = 128
HEADS = 2
WIDTH = HEADS * HD
CHUNK = 256
BLOCK = 4 * CHUNK
HEAD = 3 * CHUNK
DEPTH = 1024
SCALE = math.log2(math.e) / math.sqrt(HD)
ROW = 8
LAST = ROW - 1
LEAVE = ((3,) * 4, (5, 1, 1, 5), None, (LAST, 5, 5, LAST))

BF16 = jnp.bfloat16
F32 = jnp.float32
VMEM = pl.BlockSpec(memory_space=pltpu.VMEM)
SMEM = pl.BlockSpec(memory_space=pltpu.SMEM)
ANY = pl.BlockSpec(memory_space=pl.ANY)


def shape(rows, columns, dtype=BF16):
    return jax.ShapeDtypeStruct((rows, columns), dtype)


STATE = (shape(8, BLOCK, F32), shape(WIDTH, BLOCK, F32))


def run(name, body, out, specs, flops, *args, alias=None, scratch=(), out_specs=None):
    call = pl.pallas_call(
        body,
        out_shape=out,
        in_specs=specs,
        out_specs=out_specs or jax.tree.map(lambda _: VMEM, out),
        scratch_shapes=list(scratch),
        input_output_aliases=alias or {},
        compiler_params=pltpu.CompilerParams(vmem_limit_bytes=20 << 20),
        cost_estimate=pl.CostEstimate(flops=flops, bytes_accessed=0, transcendentals=0),
    )
    with jax.named_scope("n_" + name):
        return call(*args)


def dot(a, b, dims):
    return lax.dot_general(a, b, (dims, ((), ())), preferred_element_type=F32)


def project(rows, weight):
    return jnp.dot(rows, weight, preferred_element_type=F32).astype(BF16)


def project_query(rows, weight):
    return (jnp.dot(rows, weight, preferred_element_type=F32) * SCALE).astype(BF16)


def head(number):
    return slice(number * HD, (number + 1) * HD)


def scores(keys, query):
    return dot(keys, query, ((1,), (1,)))


def mixed(values, weights):
    return dot(values, weights.astype(BF16), ((0,), (0,)))


def positions(tp, chunks, axis):
    parts = []
    for chunk in chunks:
        size = (CHUNK, 1) if axis == 0 else (1, CHUNK)
        parts.append(lax.broadcasted_iota(jnp.int32, size, axis) + (tp ^ chunk) * CHUNK)
    return jnp.concatenate(parts, axis)


def first(found, values):
    top = jnp.max(found, axis=0, keepdims=True)
    weights = jnp.exp2(found - top)
    return top, jnp.sum(weights, axis=0, keepdims=True), mixed(values, weights)


def further(top0, total0, mix0, found, values):
    top = jnp.maximum(top0, jnp.max(found, axis=0, keepdims=True))
    weights = jnp.exp2(found - top)
    fade = jnp.exp2(top0 - top)
    total = total0 * fade + jnp.sum(weights, axis=0, keepdims=True)
    return top, total, mix0 * fade + mixed(values, weights)


def project_own_body(info, x, wq, wk, wv, q, kv):
    q[...] = project_query(x[...], wq[...])
    kv[:, :WIDTH] = project(x[...], wk[...])
    kv[:, WIDTH:] = project(x[...], wv[...])


def project_middle_body(xb, xc, qa, kva, wq, wk, wv, q, kv):
    q[:CHUNK] = qa[...]
    kv[:CHUNK] = kva[...]
    for place, x in ((1, xb), (2, xc)):
        rows = slice(place * CHUNK, (place + 1) * CHUNK)
        q[rows] = project_query(x[...], wq[...])
        kv[rows, :WIDTH] = project(x[...], wk[...])
        kv[rows, WIDTH:] = project(x[...], wv[...])


def gate_body(*refs):
    refs[-1][...] = jnp.zeros_like(refs[-1])


def project_last_body(info, passed, outer, inner, wk, wv, kv):
    def work(x):
        kv[:, :WIDTH] = project(x[...], wk[...])
        kv[:, WIDTH:] = project(x[...], wv[...])

    middle = jnp.logical_or(info[0] == 1, info[0] == 2)
    pl.when(middle)(lambda: work(inner))
    pl.when(jnp.logical_not(middle))(lambda: work(outer))


def project_far_body(info, kva, xb, xc, xd, wk, wv, kv, kvd, x, w, sems):
    @pl.when(info[2] == 1)
    def _():
        copies = [pltpu.make_async_copy(source, x.at[n], sems.at[n]) for n, source in enumerate((xb, xc, xd))]
        copies += [pltpu.make_async_copy(source, w.at[n], sems.at[3 + n]) for n, source in enumerate((wk, wv))]
        copies.append(pltpu.make_async_copy(kva, kv.at[:CHUNK], sems.at[5]))
        for copy in copies:
            copy.start()
        for copy in copies:
            copy.wait()
        for n in range(3):
            out, rows = (kv, slice((n + 1) * CHUNK, (n + 2) * CHUNK)) if n < 2 else (kvd, slice(0, CHUNK))
            out[rows, :WIDTH] = project(x[n], w[0])
            out[rows, WIDTH:] = project(x[n], w[1])


def own_first_body(info, q, kv, state, mix):
    seen = positions(info[0], range(3), 0) <= positions(info[0], range(3), 1)
    for h in range(HEADS):
        found = jnp.where(seen, scores(kv[:, head(h)], q[:, head(h)]), -jnp.inf)
        top, total, part = first(found, kv[:, head(HEADS + h)])
        state[h : h + 1, :HEAD] = top
        state[HEADS + h : HEADS + h + 1, :HEAD] = total
        mix[head(h), :HEAD] = part


def pieces(units, states):
    found = []
    for query, parts in units:
        found.append([scores(keys, query) if seen is None else jnp.where(seen, scores(keys, query), -jnp.inf) for keys, _, seen in parts])
    ready = []
    for number, tiles in enumerate(found):
        top = tiles[0].max(axis=0, keepdims=True)
        for tile in tiles[1:]:
            top = jnp.maximum(top, tile.max(axis=0, keepdims=True))
        if states[number] is not None:
            top = jnp.maximum(top, states[number][0])
        weights = [jnp.exp2(tile - top) for tile in tiles]
        total = sum(w.sum(axis=0, keepdims=True) for w in weights)
        ready.append((top, total, [w.astype(BF16) for w in weights]))
    results = []
    for number, (top, total, weights) in enumerate(ready):
        part = sum(
            dot(values, w, ((0,), (0,))) for (_, values, _), w in zip(units[number][1], weights, strict=True)
        )
        if states[number] is not None:
            top0, total0, mix0 = states[number]
            fade = jnp.exp2(top0 - top)
            total = total + total0 * fade
            part = part + mix0 * fade
        results.append((top, total, part))
    return results


def middle_body(info, outer, inner, wq, q, kv, kvd, near, far, state0, mix0, state, mix, qd, held):
    middle = jnp.logical_or(info[0] == 1, info[0] == 2)

    def query(x):
        qd[...] = project_query(x[...], wq[...])

    def hold(x):
        held[...] = x[...]

    pl.when(middle)(lambda: query(inner))
    pl.when(jnp.logical_not(middle))(lambda: query(outer))
    pl.when(info[2] == 1)(lambda: hold(far))
    pl.when(info[2] == 0)(lambda: hold(near))
    tp = info[0]
    last = tp ^ 3
    diagonal = positions(tp, (3,), 0) <= positions(tp, (3,), 1)

    def work(visible):
        for h in range(HEADS):
            k, v = head(h), head(HEADS + h)
            s, l = slice(h, h + 1), slice(HEADS + h, HEADS + h + 1)
            units, states, columns = [], [], []
            before = (held[:, k], held[:, v])
            for chunk in range(4):
                rows = slice(chunk * CHUNK, (chunk + 1) * CHUNK)
                columns.append(rows)
                if chunk < 3:
                    parts = [(kvd[:, k], kvd[:, v], last < (tp ^ chunk))]
                    states.append((state0[s, rows], state0[l, rows], mix0[k, rows]))
                else:
                    parts = [(kvd[:, k], kvd[:, v], diagonal)]
                    for other in range(3):
                        these = slice(other * CHUNK, (other + 1) * CHUNK)
                        parts.append((kv[these, k], kv[these, v], (tp ^ other) < last))
                    states.append(None)
                if visible:
                    parts.append((*before, None))
                units.append((q[rows, k] if chunk < 3 else qd[:, k], parts))
            for rows, (top, total, part) in zip(columns, pieces(units, states), strict=True):
                state[s, rows] = top
                state[l, rows] = total
                mix[k, rows] = part

    @pl.when(info[1] == 1)
    def _():
        work(True)

    @pl.when(info[1] == 0)
    def _():
        work(False)


def last_body(info, q, qd, near, far, state, mix, out, held, done, sems):
    def finish(chunk, results):
        for h, (total, part) in enumerate(results):
            held[chunk, :, head(h)] = (part / total).astype(BF16).T
        rows = pl.ds(pl.multiple_of((info[0] ^ chunk) * CHUNK, CHUNK), CHUNK)
        pltpu.make_async_copy(held.at[chunk], out.at[rows], sems.at[chunk]).start()

    @pl.when(info[2] == 1)
    def _():
        copy = pltpu.make_async_copy(far, done, sems.at[4])
        copy.start()
        copy.wait()

    @pl.when(info[2] == 0)
    def _():
        done[...] = near[...]

    @pl.when(info[1] == 1)
    def _():
        units, states = [], []
        for chunk in range(4):
            rows = slice(chunk * CHUNK, (chunk + 1) * CHUNK)
            for h in range(HEADS):
                k, v = head(h), head(HEADS + h)
                units.append((q[rows, k] if chunk < 3 else qd[:, k], [(done[:, k], done[:, v], None)]))
                states.append((state[h : h + 1, rows], state[HEADS + h : HEADS + h + 1, rows], mix[k, rows]))
        results = [(total, part) for _, total, part in pieces(units, states)]
        for chunk in range(4):
            finish(chunk, results[chunk * HEADS : (chunk + 1) * HEADS])

    @pl.when(info[1] == 0)
    def _():
        for chunk in range(4):
            rows = slice(chunk * CHUNK, (chunk + 1) * CHUNK)
            finish(chunk, [(state[HEADS + h : HEADS + h + 1, rows], mix[head(h), rows]) for h in range(HEADS)])

    for chunk in range(4):
        rows = pl.ds(pl.multiple_of((info[0] ^ chunk) * CHUNK, CHUNK), CHUNK)
        pltpu.make_async_copy(held.at[chunk], out.at[rows], sems.at[chunk]).wait()


EARLY = 20_000_000_000
FAR = 4_000_000_000
GATE = 1_000_000_000
GATE0 = 1_000_000_000
TP = 4


def device(ctx, tp):
    return ctx * TP + tp


def line_ends(ctx_count):
    return [(i, (i + ctx_count - 1) % ctx_count) for i in range(0, ctx_count, ROW)]


def body(series, w_query, w_key, w_value, block_pos):
    ctx_count = lax.axis_size("ctx")
    here = lax.axis_index("ctx")
    tp = lax.axis_index("tp")
    before = (here + ctx_count - 1) % ctx_count
    visible = block_pos[before] < block_pos[here]
    far_here = here % ROW == 0
    info = jnp.stack([tp, visible.astype(jnp.int32), far_here.astype(jnp.int32)]).astype(jnp.int32)
    weights = (w_query, w_key, w_value)
    ends = line_ends(ctx_count)

    def send(name, x, route):
        with jax.named_scope("n_" + name):
            return lax.ppermute(x, ("ctx", "tp"), route)

    def swap(name, x, pairs):
        return send(name, x, [(device(i, a), device(i, b)) for i in range(ctx_count) for a, b in pairs])

    def to_next(name, x):
        return send(name, x, [(device(i - 1, t), device(i, t)) for i in range(ctx_count) if i % ROW for t in range(TP)])

    def place(last, first, line):
        return first // (2 * ROW) * (2 * ROW) + last % (2 * ROW) - LAST + line

    def aside(name, x, places):
        return send(name, x, [(device(last, t), device(place(last, i, places[t]), t)) for i, last in ends for t in range(TP)])

    def across(name, x, chunk, places=None):
        route = []
        for i, last in ends:
            for t in range(TP):
                shard = t ^ chunk
                source = last if places is None else place(last, i, places[shard])
                route.append((device(source, shard), device(i, t)))
        return send(name, x, route)

    xc = swap("xc", series, [(t, t ^ 2) for t in range(TP)])
    xb = swap("xb", series, [(t, t ^ 1) for t in range(TP)])
    qa, kva = run(
        "own",
        project_own_body,
        (shape(CHUNK, WIDTH), shape(CHUNK, 2 * WIDTH)),
        [SMEM] + [VMEM] * 4,
        0,
        info,
        series,
        *weights,
    )
    far_c = across("across2", series, 2)
    far_b, far_d = (
        across(f"across{chunk}", aside(f"aside{chunk}", series, LEAVE[chunk]), chunk, LEAVE[chunk]) for chunk in (1, 3)
    )
    kva, far_c = lax.optimization_barrier((kva, far_c))
    far_a = across("across0", aside("aside0", kva, LEAVE[0]), 0, LEAVE[0])
    passed = run("gate0", gate_body, shape(8, 128, F32), [ANY], GATE0, xc)
    xc, own, qa, kva, passed = lax.optimization_barrier((xc, series, qa, kva, passed))
    outer = swap("outer", xc, [(2, 3), (1, 0)])
    passed = run("gate1", gate_body, shape(8, 128, F32), [ANY] * 2, GATE0, passed, far_c)
    own, far_c, passed = lax.optimization_barrier((own, far_c, passed))
    inner = swap("inner", own, [(1, 2), (2, 1)])
    q, kv = run(
        "middle",
        project_middle_body,
        (shape(HEAD, WIDTH), shape(HEAD, 2 * WIDTH)),
        [VMEM] * 7,
        0,
        xb,
        xc,
        qa,
        kva,
        *weights,
    )
    kv, far_d = lax.optimization_barrier((kv, far_d))
    near = to_next("near", kv)
    state, mix = run(
        "attend_own",
        own_first_body, STATE, [SMEM] + [VMEM] * 2, 0, info, q, kv)
    mix, far_a, far_b, far_c, far_d = lax.optimization_barrier((mix, far_a, far_b, far_c, far_d))
    far, far_last = run(
        "far",
        project_far_body,
        (shape(HEAD, 2 * WIDTH), shape(CHUNK, 2 * WIDTH)),
        [SMEM] + [ANY] * 6,
        FAR,
        info,
        far_a,
        far_b,
        far_c,
        far_d,
        w_key,
        w_value,
        scratch=(
            pltpu.VMEM((3, CHUNK, DEPTH), BF16),
            pltpu.VMEM((2, DEPTH, WIDTH), BF16),
            pltpu.SemaphoreType.DMA((6,)),
        ),
    )
    outer, far = lax.optimization_barrier((outer, far))
    passed = run("gate", gate_body, shape(8, 128, F32), [ANY] * 2, GATE, outer, passed)
    inner, passed = lax.optimization_barrier((inner, passed))
    kvd = run(
        "last",
        project_last_body,
        shape(CHUNK, 2 * WIDTH),
        [SMEM, ANY] + [VMEM] * 4,
        EARLY,
        info,
        passed,
        outer,
        inner,
        w_key,
        w_value,
    )
    near_last = to_next("near_last", kvd)
    near, kvd, outer, inner = lax.optimization_barrier((near, kvd, outer, inner))
    state, mix, qd = run(
        "attend_most",
        middle_body,
        (*STATE, shape(CHUNK, WIDTH)),
        [SMEM] + [VMEM] * 10,
        0,
        info,
        outer,
        inner,
        w_query,
        q,
        kv,
        kvd,
        near,
        far,
        state,
        mix,
        alias={9: 0, 10: 1},
        scratch=(pltpu.VMEM((HEAD, 2 * WIDTH), BF16),),
    )
    return run(
        "attend_last",
        last_body,
        shape(BLOCK, WIDTH),
        [SMEM] + [VMEM] * 3 + [ANY] + [VMEM] * 2,
        0,
        info,
        q,
        qd,
        near_last,
        far_last,
        state,
        mix,
        out_specs=ANY,
        scratch=(
            pltpu.VMEM((4, CHUNK, WIDTH), BF16),
            pltpu.VMEM((CHUNK, 2 * WIDTH), BF16),
            pltpu.SemaphoreType.DMA((5,)),
        ),
    )


def solution(mesh):
    in_specs = (P(("ctx", "tp"), None), P(None, "tp"), P(None, "tp"), P(None, "tp"), P())
    out_specs = P("ctx", "tp")
    return jax.shard_map(body, mesh=mesh, in_specs=in_specs, out_specs=out_specs, check_vma=False)
```

```python
import math

import jax
import jax.numpy as jnp
from jax import lax
from jax.experimental import pallas as pl
from jax.experimental.pallas import tpu as pltpu
from jax.sharding import PartitionSpec as P

HD = 128
HEADS = 2
WIDTH = HEADS * HD
CHUNK = 256
BLOCK = 4 * CHUNK
HEAD = 3 * CHUNK
DEPTH = 1024
SCALE = math.log2(math.e) / math.sqrt(HD)
ROW = 8
LAST = ROW - 1
LEAVE = ((1,) * 4, (5, 3, 3, 5), None, (LAST, 5, 5, LAST))

BF16 = jnp.bfloat16
F32 = jnp.float32
VMEM = pl.BlockSpec(memory_space=pltpu.VMEM)
SMEM = pl.BlockSpec(memory_space=pltpu.SMEM)
ANY = pl.BlockSpec(memory_space=pl.ANY)


def shape(rows, columns, dtype=BF16):
    return jax.ShapeDtypeStruct((rows, columns), dtype)


STATE = (shape(8, BLOCK, F32), shape(WIDTH, BLOCK, F32))


def run(name, body, out, specs, flops, *args, alias=None, scratch=(), out_specs=None):
    call = pl.pallas_call(
        body,
        out_shape=out,
        in_specs=specs,
        out_specs=out_specs or jax.tree.map(lambda _: VMEM, out),
        scratch_shapes=list(scratch),
        input_output_aliases=alias or {},
        compiler_params=pltpu.CompilerParams(vmem_limit_bytes=20 << 20),
        cost_estimate=pl.CostEstimate(flops=flops, bytes_accessed=0, transcendentals=0),
    )
    with jax.named_scope("n_" + name):
        return call(*args)


def dot(a, b, dims):
    return lax.dot_general(a, b, (dims, ((), ())), preferred_element_type=F32)


def project(rows, weight):
    return jnp.dot(rows, weight, preferred_element_type=F32).astype(BF16)


def head(number):
    return slice(number * HD, (number + 1) * HD)


def scores(keys, query):
    return dot(keys, query, ((1,), (1,))) * SCALE


def mixed(values, weights):
    return dot(values, weights.astype(BF16), ((0,), (0,)))


def positions(tp, chunks, axis):
    parts = []
    for chunk in chunks:
        size = (CHUNK, 1) if axis == 0 else (1, CHUNK)
        parts.append(lax.broadcasted_iota(jnp.int32, size, axis) + (tp ^ chunk) * CHUNK)
    return jnp.concatenate(parts, axis)


def first(found, values):
    top = jnp.max(found, axis=0, keepdims=True)
    weights = jnp.exp2(found - top)
    return top, jnp.sum(weights, axis=0, keepdims=True), mixed(values, weights)


def further(top0, total0, mix0, found, values):
    top = jnp.maximum(top0, jnp.max(found, axis=0, keepdims=True))
    weights = jnp.exp2(found - top)
    fade = jnp.exp2(top0 - top)
    total = total0 * fade + jnp.sum(weights, axis=0, keepdims=True)
    return top, total, mix0 * fade + mixed(values, weights)


def project_own_body(info, x, wq, wk, wv, q, kv):
    q[...] = project(x[...], wq[...])
    kv[:, :WIDTH] = project(x[...], wk[...])
    kv[:, WIDTH:] = project(x[...], wv[...])


def project_middle_body(xb, xc, qa, kva, wq, wk, wv, q, kv):
    q[:CHUNK] = qa[...]
    kv[:CHUNK] = kva[...]
    for place, x in ((1, xb), (2, xc)):
        rows = slice(place * CHUNK, (place + 1) * CHUNK)
        q[rows] = project(x[...], wq[...])
        kv[rows, :WIDTH] = project(x[...], wk[...])
        kv[rows, WIDTH:] = project(x[...], wv[...])


def gate_body(*refs):
    refs[-1][...] = jnp.zeros_like(refs[-1])


def project_last_body(info, passed, outer, inner, wk, wv, kv):
    def work(x):
        kv[:, :WIDTH] = project(x[...], wk[...])
        kv[:, WIDTH:] = project(x[...], wv[...])

    middle = jnp.logical_or(info[0] == 1, info[0] == 2)
    pl.when(middle)(lambda: work(inner))
    pl.when(jnp.logical_not(middle))(lambda: work(outer))


def project_far_body(info, xb, xc, xd, wk, wv, kv, kvd, x, w, sems):
    @pl.when(info[2] == 1)
    def _():
        copies = [pltpu.make_async_copy(source, x.at[n], sems.at[n]) for n, source in enumerate((xb, xc, xd))]
        copies += [pltpu.make_async_copy(source, w.at[n], sems.at[3 + n]) for n, source in enumerate((wk, wv))]
        for copy in copies:
            copy.start()
        for copy in copies:
            copy.wait()
        for n in range(3):
            out, rows = (kv, slice(n * CHUNK, (n + 1) * CHUNK)) if n < 2 else (kvd, slice(0, CHUNK))
            out[rows, :WIDTH] = project(x[n], w[0])
            out[rows, WIDTH:] = project(x[n], w[1])


def own_first_body(info, q, kv, state, mix):
    seen = positions(info[0], range(3), 0) <= positions(info[0], range(3), 1)
    for h in range(HEADS):
        found = jnp.where(seen, scores(kv[:, head(h)], q[:, head(h)]), -jnp.inf)
        top, total, part = first(found, kv[:, head(HEADS + h)])
        state[h : h + 1, :HEAD] = top
        state[HEADS + h : HEADS + h + 1, :HEAD] = total
        mix[head(h), :HEAD] = part


def pieces(units, states):
    found = []
    for query, parts in units:
        found.append([scores(keys, query) if seen is None else jnp.where(seen, scores(keys, query), -jnp.inf) for keys, _, seen in parts])
    ready = []
    for number, tiles in enumerate(found):
        top = tiles[0].max(axis=0, keepdims=True)
        for tile in tiles[1:]:
            top = jnp.maximum(top, tile.max(axis=0, keepdims=True))
        if states[number] is not None:
            top = jnp.maximum(top, states[number][0])
        weights = [jnp.exp2(tile - top) for tile in tiles]
        total = sum(w.sum(axis=0, keepdims=True) for w in weights)
        ready.append((top, total, [w.astype(BF16) for w in weights]))
    results = []
    for number, (top, total, weights) in enumerate(ready):
        part = sum(
            dot(values, w, ((0,), (0,))) for (_, values, _), w in zip(units[number][1], weights, strict=True)
        )
        if states[number] is not None:
            top0, total0, mix0 = states[number]
            fade = jnp.exp2(top0 - top)
            total = total + total0 * fade
            part = part + mix0 * fade
        results.append((top, total, part))
    return results


def middle_body(info, outer, inner, wq, q, kv, kvd, near, far_a, far, state0, mix0, state, mix, qd, held):
    middle = jnp.logical_or(info[0] == 1, info[0] == 2)

    def query(x):
        qd[...] = project(x[...], wq[...])

    def hold(*parts):
        start = 0
        for part in parts:
            held[start : start + part.shape[0]] = part[...]
            start += part.shape[0]

    pl.when(middle)(lambda: query(inner))
    pl.when(jnp.logical_not(middle))(lambda: query(outer))
    pl.when(info[2] == 1)(lambda: hold(far_a, far))
    pl.when(info[2] == 0)(lambda: hold(near))
    tp = info[0]
    last = tp ^ 3
    diagonal = positions(tp, (3,), 0) <= positions(tp, (3,), 1)

    def work(visible):
        for h in range(HEADS):
            k, v = head(h), head(HEADS + h)
            s, l = slice(h, h + 1), slice(HEADS + h, HEADS + h + 1)
            units, states, columns = [], [], []
            before = (held[:, k], held[:, v])
            for chunk in range(4):
                rows = slice(chunk * CHUNK, (chunk + 1) * CHUNK)
                columns.append(rows)
                if chunk < 3:
                    parts = [(kvd[:, k], kvd[:, v], last < (tp ^ chunk))]
                    states.append((state0[s, rows], state0[l, rows], mix0[k, rows]))
                else:
                    parts = [(kvd[:, k], kvd[:, v], diagonal)]
                    for other in range(3):
                        these = slice(other * CHUNK, (other + 1) * CHUNK)
                        parts.append((kv[these, k], kv[these, v], (tp ^ other) < last))
                    states.append(None)
                if visible:
                    parts.append((*before, None))
                units.append((q[rows, k] if chunk < 3 else qd[:, k], parts))
            for rows, (top, total, part) in zip(columns, pieces(units, states), strict=True):
                state[s, rows] = top
                state[l, rows] = total
                mix[k, rows] = part

    @pl.when(info[1] == 1)
    def _():
        work(True)

    @pl.when(info[1] == 0)
    def _():
        work(False)


def last_body(info, q, qd, near, far, state, mix, out, held, done, sems):
    def finish(chunk, results):
        for h, (total, part) in enumerate(results):
            held[chunk, :, head(h)] = (part / total).astype(BF16).T
        rows = pl.ds(pl.multiple_of((info[0] ^ chunk) * CHUNK, CHUNK), CHUNK)
        pltpu.make_async_copy(held.at[chunk], out.at[rows], sems.at[chunk]).start()

    @pl.when(info[2] == 1)
    def _():
        copy = pltpu.make_async_copy(far, done, sems.at[4])
        copy.start()
        copy.wait()

    @pl.when(info[2] == 0)
    def _():
        done[...] = near[...]

    @pl.when(info[1] == 1)
    def _():
        units, states = [], []
        for chunk in range(4):
            rows = slice(chunk * CHUNK, (chunk + 1) * CHUNK)
            for h in range(HEADS):
                k, v = head(h), head(HEADS + h)
                units.append((q[rows, k] if chunk < 3 else qd[:, k], [(done[:, k], done[:, v], None)]))
                states.append((state[h : h + 1, rows], state[HEADS + h : HEADS + h + 1, rows], mix[k, rows]))
        results = [(total, part) for _, total, part in pieces(units, states)]
        for chunk in range(4):
            finish(chunk, results[chunk * HEADS : (chunk + 1) * HEADS])

    @pl.when(info[1] == 0)
    def _():
        for chunk in range(4):
            rows = slice(chunk * CHUNK, (chunk + 1) * CHUNK)
            finish(chunk, [(state[HEADS + h : HEADS + h + 1, rows], mix[head(h), rows]) for h in range(HEADS)])

    for chunk in range(4):
        rows = pl.ds(pl.multiple_of((info[0] ^ chunk) * CHUNK, CHUNK), CHUNK)
        pltpu.make_async_copy(held.at[chunk], out.at[rows], sems.at[chunk]).wait()


EARLY = 20_000_000_000
FAR = 4_000_000_000
GATE = 1_000_000_000
GATE0 = 1_000_000_000
TP = 4


def device(ctx, tp):
    return ctx * TP + tp


def line_ends(ctx_count):
    return [(i, (i + ctx_count - 1) % ctx_count) for i in range(0, ctx_count, ROW)]


def body(series, w_query, w_key, w_value, block_pos):
    ctx_count = lax.axis_size("ctx")
    here = lax.axis_index("ctx")
    tp = lax.axis_index("tp")
    before = (here + ctx_count - 1) % ctx_count
    visible = block_pos[before] < block_pos[here]
    far_here = here % ROW == 0
    info = jnp.stack([tp, visible.astype(jnp.int32), far_here.astype(jnp.int32)]).astype(jnp.int32)
    weights = (w_query, w_key, w_value)
    ends = line_ends(ctx_count)

    def send(name, x, route):
        with jax.named_scope("n_" + name):
            return lax.ppermute(x, ("ctx", "tp"), route)

    def swap(name, x, pairs):
        return send(name, x, [(device(i, a), device(i, b)) for i in range(ctx_count) for a, b in pairs])

    def to_next(name, x):
        return send(name, x, [(device(i - 1, t), device(i, t)) for i in range(ctx_count) if i % ROW for t in range(TP)])

    def place(last, first, line):
        return first // (2 * ROW) * (2 * ROW) + last % (2 * ROW) - LAST + line

    def aside(name, x, places):
        return send(name, x, [(device(last, t), device(place(last, i, places[t]), t)) for i, last in ends for t in range(TP)])

    def across(name, x, chunk, places=None):
        route = []
        for i, last in ends:
            for t in range(TP):
                shard = t ^ chunk
                source = last if places is None else place(last, i, places[shard])
                route.append((device(source, shard), device(i, t)))
        return send(name, x, route)

    xc = swap("xc", series, [(t, t ^ 2) for t in range(TP)])
    xb = swap("xb", series, [(t, t ^ 1) for t in range(TP)])
    qa, kva = run(
        "own",
        project_own_body,
        (shape(CHUNK, WIDTH), shape(CHUNK, 2 * WIDTH)),
        [SMEM] + [VMEM] * 4,
        0,
        info,
        series,
        *weights,
    )
    far_c = across("across2", series, 2)
    far_b, far_d = (
        across(f"across{chunk}", aside(f"aside{chunk}", series, LEAVE[chunk]), chunk, LEAVE[chunk]) for chunk in (1, 3)
    )
    kva, far_c = lax.optimization_barrier((kva, far_c))
    far_a = across("across0", aside("aside0", kva, LEAVE[0]), 0, LEAVE[0])
    passed = run("gate0", gate_body, shape(8, 128, F32), [ANY], GATE0, xc)
    xc, own, qa, kva, passed = lax.optimization_barrier((xc, series, qa, kva, passed))
    outer = swap("outer", xc, [(2, 3), (1, 0)])
    passed = run("gate1", gate_body, shape(8, 128, F32), [ANY] * 2, GATE0, passed, far_c)
    own, far_c, passed = lax.optimization_barrier((own, far_c, passed))
    inner = swap("inner", own, [(1, 2), (2, 1)])
    q, kv = run(
        "middle",
        project_middle_body,
        (shape(HEAD, WIDTH), shape(HEAD, 2 * WIDTH)),
        [VMEM] * 7,
        0,
        xb,
        xc,
        qa,
        kva,
        *weights,
    )
    kv, far_d = lax.optimization_barrier((kv, far_d))
    near = to_next("near", kv)
    state, mix = run(
        "attend_own",
        own_first_body, STATE, [SMEM] + [VMEM] * 2, 0, info, q, kv)
    mix, far_b, far_c, far_d = lax.optimization_barrier((mix, far_b, far_c, far_d))
    far, far_last = run(
        "far",
        project_far_body,
        (shape(2 * CHUNK, 2 * WIDTH), shape(CHUNK, 2 * WIDTH)),
        [SMEM] + [ANY] * 5,
        FAR,
        info,
        far_b,
        far_c,
        far_d,
        w_key,
        w_value,
        scratch=(
            pltpu.VMEM((3, CHUNK, DEPTH), BF16),
            pltpu.VMEM((2, DEPTH, WIDTH), BF16),
            pltpu.SemaphoreType.DMA((5,)),
        ),
    )
    outer, far, far_a = lax.optimization_barrier((outer, far, far_a))
    passed = run("gate", gate_body, shape(8, 128, F32), [ANY] * 2, GATE, outer, passed)
    inner, passed = lax.optimization_barrier((inner, passed))
    kvd = run(
        "last",
        project_last_body,
        shape(CHUNK, 2 * WIDTH),
        [SMEM, ANY] + [VMEM] * 4,
        EARLY,
        info,
        passed,
        outer,
        inner,
        w_key,
        w_value,
    )
    near_last = to_next("near_last", kvd)
    near, kvd, outer, inner = lax.optimization_barrier((near, kvd, outer, inner))
    state, mix, qd = run(
        "attend_most",
        middle_body,
        (*STATE, shape(CHUNK, WIDTH)),
        [SMEM] + [VMEM] * 11,
        0,
        info,
        outer,
        inner,
        w_query,
        q,
        kv,
        kvd,
        near,
        far_a,
        far,
        state,
        mix,
        alias={10: 0, 11: 1},
        scratch=(pltpu.VMEM((HEAD, 2 * WIDTH), BF16),),
    )
    return run(
        "attend_last",
        last_body,
        shape(BLOCK, WIDTH),
        [SMEM] + [VMEM] * 3 + [ANY] + [VMEM] * 2,
        0,
        info,
        q,
        qd,
        near_last,
        far_last,
        state,
        mix,
        out_specs=ANY,
        scratch=(
            pltpu.VMEM((4, CHUNK, WIDTH), BF16),
            pltpu.VMEM((CHUNK, 2 * WIDTH), BF16),
            pltpu.SemaphoreType.DMA((5,)),
        ),
    )


def solution(mesh):
    in_specs = (P(("ctx", "tp"), None), P(None, "tp"), P(None, "tp"), P(None, "tp"), P())
    out_specs = P("ctx", "tp")
    return jax.shard_map(body, mesh=mesh, in_specs=in_specs, out_specs=out_specs, check_vma=False)
```

```python
import math

import jax
import jax.numpy as jnp
from jax import lax
from jax.experimental import pallas as pl
from jax.experimental.pallas import tpu as pltpu
from jax.sharding import PartitionSpec as P

HD = 128
HEADS = 2
WIDTH = HEADS * HD
CHUNK = 256
BLOCK = 4 * CHUNK
HEAD = 3 * CHUNK
DEPTH = 1024
SCALE = math.log2(math.e) / math.sqrt(HD)
ROW = 8
LAST = ROW - 1
LEAVE = ((1,) * 4, (5, 3, 3, 5), None, (LAST, 1, 1, LAST))

BF16 = jnp.bfloat16
F32 = jnp.float32
VMEM = pl.BlockSpec(memory_space=pltpu.VMEM)
SMEM = pl.BlockSpec(memory_space=pltpu.SMEM)
ANY = pl.BlockSpec(memory_space=pl.ANY)


def shape(rows, columns, dtype=BF16):
    return jax.ShapeDtypeStruct((rows, columns), dtype)


STATE = (shape(8, BLOCK, F32), shape(WIDTH, BLOCK, F32))


def run(name, body, out, specs, flops, *args, alias=None, scratch=(), out_specs=None):
    call = pl.pallas_call(
        body,
        out_shape=out,
        in_specs=specs,
        out_specs=out_specs or jax.tree.map(lambda _: VMEM, out),
        scratch_shapes=list(scratch),
        input_output_aliases=alias or {},
        compiler_params=pltpu.CompilerParams(vmem_limit_bytes=20 << 20),
        cost_estimate=pl.CostEstimate(flops=flops, bytes_accessed=0, transcendentals=0),
    )
    with jax.named_scope("n_" + name):
        return call(*args)


def dot(a, b, dims):
    return lax.dot_general(a, b, (dims, ((), ())), preferred_element_type=F32)


def project(rows, weight):
    return jnp.dot(rows, weight, preferred_element_type=F32).astype(BF16)


def head(number):
    return slice(number * HD, (number + 1) * HD)


def scores(keys, query):
    return dot(keys, query, ((1,), (1,))) * SCALE


def mixed(values, weights):
    return dot(values, weights.astype(BF16), ((0,), (0,)))


def positions(tp, chunks, axis):
    parts = []
    for chunk in chunks:
        size = (CHUNK, 1) if axis == 0 else (1, CHUNK)
        parts.append(lax.broadcasted_iota(jnp.int32, size, axis) + (tp ^ chunk) * CHUNK)
    return jnp.concatenate(parts, axis)


def first(found, values):
    top = jnp.max(found, axis=0, keepdims=True)
    weights = jnp.exp2(found - top)
    return top, jnp.sum(weights, axis=0, keepdims=True), mixed(values, weights)


def further(top0, total0, mix0, found, values):
    top = jnp.maximum(top0, jnp.max(found, axis=0, keepdims=True))
    weights = jnp.exp2(found - top)
    fade = jnp.exp2(top0 - top)
    total = total0 * fade + jnp.sum(weights, axis=0, keepdims=True)
    return top, total, mix0 * fade + mixed(values, weights)


def project_own_body(info, x, wq, wk, wv, q, kv):
    q[...] = project(x[...], wq[...])
    kv[:, :WIDTH] = project(x[...], wk[...])
    kv[:, WIDTH:] = project(x[...], wv[...])


def project_middle_body(xb, xc, qa, kva, wq, wk, wv, q, kv):
    q[:CHUNK] = qa[...]
    kv[:CHUNK] = kva[...]
    for place, x in ((1, xb), (2, xc)):
        rows = slice(place * CHUNK, (place + 1) * CHUNK)
        q[rows] = project(x[...], wq[...])
        kv[rows, :WIDTH] = project(x[...], wk[...])
        kv[rows, WIDTH:] = project(x[...], wv[...])


def gate_body(*refs):
    refs[-1][...] = jnp.zeros_like(refs[-1])


def project_last_body(info, passed, outer, inner, wk, wv, kv):
    def work(x):
        kv[:, :WIDTH] = project(x[...], wk[...])
        kv[:, WIDTH:] = project(x[...], wv[...])

    middle = jnp.logical_or(info[0] == 1, info[0] == 2)
    pl.when(middle)(lambda: work(inner))
    pl.when(jnp.logical_not(middle))(lambda: work(outer))


def project_far_body(info, xb, xc, xd, wk, wv, kv, kvd, x, w, sems):
    @pl.when(info[2] == 1)
    def _():
        copies = [pltpu.make_async_copy(source, x.at[n], sems.at[n]) for n, source in enumerate((xb, xc, xd))]
        copies += [pltpu.make_async_copy(source, w.at[n], sems.at[3 + n]) for n, source in enumerate((wk, wv))]
        for copy in copies:
            copy.start()
        for copy in copies:
            copy.wait()
        for n in range(3):
            out, rows = (kv, slice(n * CHUNK, (n + 1) * CHUNK)) if n < 2 else (kvd, slice(0, CHUNK))
            out[rows, :WIDTH] = project(x[n], w[0])
            out[rows, WIDTH:] = project(x[n], w[1])


def own_first_body(info, q, kv, state, mix):
    seen = positions(info[0], range(3), 0) <= positions(info[0], range(3), 1)
    for h in range(HEADS):
        found = jnp.where(seen, scores(kv[:, head(h)], q[:, head(h)]), -jnp.inf)
        top, total, part = first(found, kv[:, head(HEADS + h)])
        state[h : h + 1, :HEAD] = top
        state[HEADS + h : HEADS + h + 1, :HEAD] = total
        mix[head(h), :HEAD] = part


def pieces(units, states):
    found = []
    for query, parts in units:
        found.append([scores(keys, query) if seen is None else jnp.where(seen, scores(keys, query), -jnp.inf) for keys, _, seen in parts])
    ready = []
    for number, tiles in enumerate(found):
        top = tiles[0].max(axis=0, keepdims=True)
        for tile in tiles[1:]:
            top = jnp.maximum(top, tile.max(axis=0, keepdims=True))
        if states[number] is not None:
            top = jnp.maximum(top, states[number][0])
        weights = [jnp.exp2(tile - top) for tile in tiles]
        total = sum(w.sum(axis=0, keepdims=True) for w in weights)
        ready.append((top, total, [w.astype(BF16) for w in weights]))
    results = []
    for number, (top, total, weights) in enumerate(ready):
        part = sum(
            dot(values, w, ((0,), (0,))) for (_, values, _), w in zip(units[number][1], weights, strict=True)
        )
        if states[number] is not None:
            top0, total0, mix0 = states[number]
            fade = jnp.exp2(top0 - top)
            total = total + total0 * fade
            part = part + mix0 * fade
        results.append((top, total, part))
    return results


def middle_body(info, passed, outer, inner, wq, q, kv, kvd, near, far_a, far, state0, mix0, state, mix, qd, held):
    middle = jnp.logical_or(info[0] == 1, info[0] == 2)

    def query(x):
        qd[...] = project(x[...], wq[...])

    def hold(*parts):
        start = 0
        for part in parts:
            held[start : start + part.shape[0]] = part[...]
            start += part.shape[0]

    pl.when(middle)(lambda: query(inner))
    pl.when(jnp.logical_not(middle))(lambda: query(outer))
    pl.when(info[2] == 1)(lambda: hold(far_a, far))
    pl.when(info[2] == 0)(lambda: hold(near))
    tp = info[0]
    last = tp ^ 3
    diagonal = positions(tp, (3,), 0) <= positions(tp, (3,), 1)

    def work(visible):
        for h in range(HEADS):
            k, v = head(h), head(HEADS + h)
            s, l = slice(h, h + 1), slice(HEADS + h, HEADS + h + 1)
            units, states, columns = [], [], []
            before = (held[:, k], held[:, v])
            for chunk in range(4):
                rows = slice(chunk * CHUNK, (chunk + 1) * CHUNK)
                columns.append(rows)
                if chunk < 3:
                    parts = [(kvd[:, k], kvd[:, v], last < (tp ^ chunk))]
                    states.append((state0[s, rows], state0[l, rows], mix0[k, rows]))
                else:
                    parts = [(kvd[:, k], kvd[:, v], diagonal)]
                    for other in range(3):
                        these = slice(other * CHUNK, (other + 1) * CHUNK)
                        parts.append((kv[these, k], kv[these, v], (tp ^ other) < last))
                    states.append(None)
                if visible:
                    parts.append((*before, None))
                units.append((q[rows, k] if chunk < 3 else qd[:, k], parts))
            for rows, (top, total, part) in zip(columns, pieces(units, states), strict=True):
                state[s, rows] = top
                state[l, rows] = total
                mix[k, rows] = part

    @pl.when(info[1] == 1)
    def _():
        work(True)

    @pl.when(info[1] == 0)
    def _():
        work(False)


def last_body(info, q, qd, near, far, state, mix, out, held, done, sems):
    def finish(chunk, results):
        for h, (total, part) in enumerate(results):
            held[chunk, :, head(h)] = (part / total).astype(BF16).T
        rows = pl.ds(pl.multiple_of((info[0] ^ chunk) * CHUNK, CHUNK), CHUNK)
        pltpu.make_async_copy(held.at[chunk], out.at[rows], sems.at[chunk]).start()

    @pl.when(info[2] == 1)
    def _():
        copy = pltpu.make_async_copy(far, done, sems.at[4])
        copy.start()
        copy.wait()

    @pl.when(info[2] == 0)
    def _():
        done[...] = near[...]

    @pl.when(info[1] == 1)
    def _():
        units, states = [], []
        for chunk in range(4):
            rows = slice(chunk * CHUNK, (chunk + 1) * CHUNK)
            for h in range(HEADS):
                k, v = head(h), head(HEADS + h)
                units.append((q[rows, k] if chunk < 3 else qd[:, k], [(done[:, k], done[:, v], None)]))
                states.append((state[h : h + 1, rows], state[HEADS + h : HEADS + h + 1, rows], mix[k, rows]))
        results = [(total, part) for _, total, part in pieces(units, states)]
        for chunk in range(4):
            finish(chunk, results[chunk * HEADS : (chunk + 1) * HEADS])

    @pl.when(info[1] == 0)
    def _():
        for chunk in range(4):
            rows = slice(chunk * CHUNK, (chunk + 1) * CHUNK)
            finish(chunk, [(state[HEADS + h : HEADS + h + 1, rows], mix[head(h), rows]) for h in range(HEADS)])

    for chunk in range(4):
        rows = pl.ds(pl.multiple_of((info[0] ^ chunk) * CHUNK, CHUNK), CHUNK)
        pltpu.make_async_copy(held.at[chunk], out.at[rows], sems.at[chunk]).wait()


EARLY = 20_000_000_000
FAR = 4_000_000_000
GATE = 1_000_000_000
GATE0 = 1_000_000_000
TP = 4


def device(ctx, tp):
    return ctx * TP + tp


def line_ends(ctx_count):
    return [(i, (i + ctx_count - 1) % ctx_count) for i in range(0, ctx_count, ROW)]


def body(series, w_query, w_key, w_value, block_pos):
    ctx_count = lax.axis_size("ctx")
    here = lax.axis_index("ctx")
    tp = lax.axis_index("tp")
    before = (here + ctx_count - 1) % ctx_count
    visible = block_pos[before] < block_pos[here]
    far_here = here % ROW == 0
    info = jnp.stack([tp, visible.astype(jnp.int32), far_here.astype(jnp.int32)]).astype(jnp.int32)
    weights = (w_query, w_key, w_value)
    ends = line_ends(ctx_count)

    def send(name, x, route):
        with jax.named_scope("n_" + name):
            return lax.ppermute(x, ("ctx", "tp"), route)

    def swap(name, x, pairs):
        return send(name, x, [(device(i, a), device(i, b)) for i in range(ctx_count) for a, b in pairs])

    def to_next(name, x):
        return send(name, x, [(device(i - 1, t), device(i, t)) for i in range(ctx_count) if i % ROW for t in range(TP)])

    def place(last, first, line):
        return first // (2 * ROW) * (2 * ROW) + last % (2 * ROW) - LAST + line

    def aside(name, x, places):
        return send(name, x, [(device(last, t), device(place(last, i, places[t]), t)) for i, last in ends for t in range(TP)])

    def across(name, x, chunk, places=None):
        route = []
        for i, last in ends:
            for t in range(TP):
                shard = t ^ chunk
                source = last if places is None else place(last, i, places[shard])
                route.append((device(source, shard), device(i, t)))
        return send(name, x, route)

    xc = swap("xc", series, [(t, t ^ 2) for t in range(TP)])
    xb = swap("xb", series, [(t, t ^ 1) for t in range(TP)])
    qa, kva = run(
        "own",
        project_own_body,
        (shape(CHUNK, WIDTH), shape(CHUNK, 2 * WIDTH)),
        [SMEM] + [VMEM] * 4,
        0,
        info,
        series,
        *weights,
    )
    far_c = across("across2", series, 2)
    far_b, far_d = (
        across(f"across{chunk}", aside(f"aside{chunk}", series, LEAVE[chunk]), chunk, LEAVE[chunk]) for chunk in (1, 3)
    )
    kva, far_c = lax.optimization_barrier((kva, far_c))
    far_a = across("across0", aside("aside0", kva, LEAVE[0]), 0, LEAVE[0])
    passed = run("gate0", gate_body, shape(8, 128, F32), [ANY], GATE0, xc)
    xc, own, qa, kva, passed = lax.optimization_barrier((xc, series, qa, kva, passed))
    outer = swap("outer", xc, [(2, 3), (1, 0)])
    passed = run("gate1", gate_body, shape(8, 128, F32), [ANY] * 2, GATE0, passed, far_c)
    own, far_c, passed = lax.optimization_barrier((own, far_c, passed))
    inner = swap("inner", own, [(1, 2), (2, 1)])
    q, kv = run(
        "middle",
        project_middle_body,
        (shape(HEAD, WIDTH), shape(HEAD, 2 * WIDTH)),
        [VMEM] * 7,
        0,
        xb,
        xc,
        qa,
        kva,
        *weights,
    )
    kv, far_d = lax.optimization_barrier((kv, far_d))
    near = to_next("near", kv)
    state, mix = run(
        "attend_own",
        own_first_body, STATE, [SMEM] + [VMEM] * 2, 0, info, q, kv)
    mix, far_b, far_c, far_d = lax.optimization_barrier((mix, far_b, far_c, far_d))
    far, far_last = run(
        "far",
        project_far_body,
        (shape(2 * CHUNK, 2 * WIDTH), shape(CHUNK, 2 * WIDTH)),
        [SMEM] + [ANY] * 5,
        FAR,
        info,
        far_b,
        far_c,
        far_d,
        w_key,
        w_value,
        scratch=(
            pltpu.VMEM((3, CHUNK, DEPTH), BF16),
            pltpu.VMEM((2, DEPTH, WIDTH), BF16),
            pltpu.SemaphoreType.DMA((5,)),
        ),
    )
    outer, far = lax.optimization_barrier((outer, far))
    passed = run("gate", gate_body, shape(8, 128, F32), [ANY] * 2, GATE, outer, passed)
    inner, passed = lax.optimization_barrier((inner, passed))
    kvd = run(
        "last",
        project_last_body,
        shape(CHUNK, 2 * WIDTH),
        [SMEM, ANY] + [VMEM] * 4,
        0,
        info,
        passed,
        outer,
        inner,
        w_key,
        w_value,
    )
    near_last = to_next("near_last", kvd)
    passed = run("gate2", gate_body, shape(8, 128, F32), [ANY] * 2, EARLY, kvd, far_a)
    near, kvd, outer, inner, passed = lax.optimization_barrier((near, kvd, outer, inner, passed))
    state, mix, qd = run(
        "attend_most",
        middle_body,
        (*STATE, shape(CHUNK, WIDTH)),
        [SMEM, ANY] + [VMEM] * 11,
        0,
        info,
        passed,
        outer,
        inner,
        w_query,
        q,
        kv,
        kvd,
        near,
        far_a,
        far,
        state,
        mix,
        alias={11: 0, 12: 1},
        scratch=(pltpu.VMEM((HEAD, 2 * WIDTH), BF16),),
    )
    return run(
        "attend_last",
        last_body,
        shape(BLOCK, WIDTH),
        [SMEM] + [VMEM] * 3 + [ANY] + [VMEM] * 2,
        0,
        info,
        q,
        qd,
        near_last,
        far_last,
        state,
        mix,
        out_specs=ANY,
        scratch=(
            pltpu.VMEM((4, CHUNK, WIDTH), BF16),
            pltpu.VMEM((CHUNK, 2 * WIDTH), BF16),
            pltpu.SemaphoreType.DMA((5,)),
        ),
    )


def solution(mesh):
    in_specs = (P(("ctx", "tp"), None), P(None, "tp"), P(None, "tp"), P(None, "tp"), P())
    out_specs = P("ctx", "tp")
    return jax.shard_map(body, mesh=mesh, in_specs=in_specs, out_specs=out_specs, check_vma=False)
```

```python
import math

import jax
import jax.numpy as jnp
from jax import lax
from jax.experimental import pallas as pl
from jax.experimental.pallas import tpu as pltpu
from jax.sharding import PartitionSpec as P

HD = 128
HEADS = 2
WIDTH = HEADS * HD
CHUNK = 256
BLOCK = 4 * CHUNK
HEAD = 3 * CHUNK
DEPTH = 1024
SCALE = math.log2(math.e) / math.sqrt(HD)
ROW = 8
LAST = ROW - 1
LEAVE = ((1,) * 4, (5, 3, 3, 5), None, (LAST, 1, 1, LAST))

BF16 = jnp.bfloat16
F32 = jnp.float32
VMEM = pl.BlockSpec(memory_space=pltpu.VMEM)
SMEM = pl.BlockSpec(memory_space=pltpu.SMEM)
ANY = pl.BlockSpec(memory_space=pl.ANY)


def shape(rows, columns, dtype=BF16):
    return jax.ShapeDtypeStruct((rows, columns), dtype)


STATE = (shape(8, BLOCK, F32), shape(WIDTH, BLOCK, F32))


def run(name, body, out, specs, flops, *args, alias=None, scratch=(), out_specs=None):
    call = pl.pallas_call(
        body,
        out_shape=out,
        in_specs=specs,
        out_specs=out_specs or jax.tree.map(lambda _: VMEM, out),
        scratch_shapes=list(scratch),
        input_output_aliases=alias or {},
        compiler_params=pltpu.CompilerParams(vmem_limit_bytes=20 << 20),
        cost_estimate=pl.CostEstimate(flops=flops, bytes_accessed=0, transcendentals=0),
    )
    with jax.named_scope("n_" + name):
        return call(*args)


def dot(a, b, dims):
    return lax.dot_general(a, b, (dims, ((), ())), preferred_element_type=F32)


def project(rows, weight):
    return jnp.dot(rows, weight, preferred_element_type=F32).astype(BF16)


def head(number):
    return slice(number * HD, (number + 1) * HD)


def scores(keys, query):
    return dot(keys, query, ((1,), (1,))) * SCALE


def mixed(values, weights):
    return dot(values, weights.astype(BF16), ((0,), (0,)))


def positions(tp, chunks, axis):
    parts = []
    for chunk in chunks:
        size = (CHUNK, 1) if axis == 0 else (1, CHUNK)
        parts.append(lax.broadcasted_iota(jnp.int32, size, axis) + (tp ^ chunk) * CHUNK)
    return jnp.concatenate(parts, axis)


def first(found, values):
    top = jnp.max(found, axis=0, keepdims=True)
    weights = jnp.exp2(found - top)
    return top, jnp.sum(weights, axis=0, keepdims=True), mixed(values, weights)


def further(top0, total0, mix0, found, values):
    top = jnp.maximum(top0, jnp.max(found, axis=0, keepdims=True))
    weights = jnp.exp2(found - top)
    fade = jnp.exp2(top0 - top)
    total = total0 * fade + jnp.sum(weights, axis=0, keepdims=True)
    return top, total, mix0 * fade + mixed(values, weights)


def project_own_body(info, x, wq, wk, wv, q, kv):
    q[...] = project(x[...], wq[...])
    kv[:, :WIDTH] = project(x[...], wk[...])
    kv[:, WIDTH:] = project(x[...], wv[...])


def project_middle_body(xb, xc, qa, kva, wq, wk, wv, q, kv):
    q[:CHUNK] = qa[...]
    kv[:CHUNK] = kva[...]
    for place, x in ((1, xb), (2, xc)):
        rows = slice(place * CHUNK, (place + 1) * CHUNK)
        q[rows] = project(x[...], wq[...])
        kv[rows, :WIDTH] = project(x[...], wk[...])
        kv[rows, WIDTH:] = project(x[...], wv[...])


def gate_body(*refs):
    refs[-1][...] = jnp.zeros_like(refs[-1])


def project_last_body(info, passed, outer, inner, wk, wv, kv):
    def work(x):
        kv[:, :WIDTH] = project(x[...], wk[...])
        kv[:, WIDTH:] = project(x[...], wv[...])

    middle = jnp.logical_or(info[0] == 1, info[0] == 2)
    pl.when(middle)(lambda: work(inner))
    pl.when(jnp.logical_not(middle))(lambda: work(outer))


def project_far_body(info, xb, xc, xd, wk, wv, kv, kvd, x, w, sems):
    @pl.when(info[2] == 1)
    def _():
        copies = [pltpu.make_async_copy(source, x.at[n], sems.at[n]) for n, source in enumerate((xb, xc, xd))]
        copies += [pltpu.make_async_copy(source, w.at[n], sems.at[3 + n]) for n, source in enumerate((wk, wv))]
        for copy in copies:
            copy.start()
        for copy in copies:
            copy.wait()
        for n in range(3):
            out, rows = (kv, slice(n * CHUNK, (n + 1) * CHUNK)) if n < 2 else (kvd, slice(0, CHUNK))
            out[rows, :WIDTH] = project(x[n], w[0])
            out[rows, WIDTH:] = project(x[n], w[1])


def own_first_body(info, q, kv, state, mix):
    seen = positions(info[0], range(3), 0) <= positions(info[0], range(3), 1)
    for h in range(HEADS):
        found = jnp.where(seen, scores(kv[:, head(h)], q[:, head(h)]), -jnp.inf)
        top, total, part = first(found, kv[:, head(HEADS + h)])
        state[h : h + 1, :HEAD] = top
        state[HEADS + h : HEADS + h + 1, :HEAD] = total
        mix[head(h), :HEAD] = part


def pieces(units, states):
    found = []
    for query, parts in units:
        found.append([scores(keys, query) if seen is None else jnp.where(seen, scores(keys, query), -jnp.inf) for keys, _, seen in parts])
    ready = []
    for number, tiles in enumerate(found):
        top = tiles[0].max(axis=0, keepdims=True)
        for tile in tiles[1:]:
            top = jnp.maximum(top, tile.max(axis=0, keepdims=True))
        if states[number] is not None:
            top = jnp.maximum(top, states[number][0])
        weights = [jnp.exp2(tile - top) for tile in tiles]
        total = sum(w.sum(axis=0, keepdims=True) for w in weights)
        ready.append((top, total, [w.astype(BF16) for w in weights]))
    results = []
    for number, (top, total, weights) in enumerate(ready):
        part = sum(
            dot(values, w, ((0,), (0,))) for (_, values, _), w in zip(units[number][1], weights, strict=True)
        )
        if states[number] is not None:
            top0, total0, mix0 = states[number]
            fade = jnp.exp2(top0 - top)
            total = total + total0 * fade
            part = part + mix0 * fade
        results.append((top, total, part))
    return results


def middle_body(info, passed, outer, inner, wq, q, kv, kvd, near, far_a, far, state0, mix0, state, mix, qd, held):
    middle = jnp.logical_or(info[0] == 1, info[0] == 2)

    def query(x):
        qd[...] = project(x[...], wq[...])

    def hold(*parts):
        start = 0
        for part in parts:
            held[start : start + part.shape[0]] = part[...]
            start += part.shape[0]

    pl.when(middle)(lambda: query(inner))
    pl.when(jnp.logical_not(middle))(lambda: query(outer))
    pl.when(info[2] == 1)(lambda: hold(far_a, far))
    pl.when(info[2] == 0)(lambda: hold(near))
    tp = info[0]
    last = tp ^ 3
    diagonal = positions(tp, (3,), 0) <= positions(tp, (3,), 1)

    def work(visible):
        units, states, places = [], [], []
        for h in range(HEADS):
            k, v = head(h), head(HEADS + h)
            s, l = slice(h, h + 1), slice(HEADS + h, HEADS + h + 1)
            before = (held[:, k], held[:, v])
            for chunk in range(4):
                rows = slice(chunk * CHUNK, (chunk + 1) * CHUNK)
                places.append((s, l, k, rows))
                if chunk < 3:
                    parts = [(kvd[:, k], kvd[:, v], last < (tp ^ chunk))]
                    states.append((state0[s, rows], state0[l, rows], mix0[k, rows]))
                else:
                    parts = [(kvd[:, k], kvd[:, v], diagonal)]
                    for other in range(3):
                        these = slice(other * CHUNK, (other + 1) * CHUNK)
                        parts.append((kv[these, k], kv[these, v], (tp ^ other) < last))
                    states.append(None)
                if visible:
                    parts.append((*before, None))
                units.append((q[rows, k] if chunk < 3 else qd[:, k], parts))
        for (s, l, k, rows), (top, total, part) in zip(places, pieces(units, states), strict=True):
            state[s, rows] = top
            state[l, rows] = total
            mix[k, rows] = part

    @pl.when(info[1] == 1)
    def _():
        work(True)

    @pl.when(info[1] == 0)
    def _():
        work(False)


def last_body(info, q, qd, near, far, state, mix, out, held, done, sems):
    def finish(chunk, results):
        for h, (total, part) in enumerate(results):
            held[chunk, :, head(h)] = (part / total).astype(BF16).T
        rows = pl.ds(pl.multiple_of((info[0] ^ chunk) * CHUNK, CHUNK), CHUNK)
        pltpu.make_async_copy(held.at[chunk], out.at[rows], sems.at[chunk]).start()

    @pl.when(info[2] == 1)
    def _():
        copy = pltpu.make_async_copy(far, done, sems.at[4])
        copy.start()
        copy.wait()

    @pl.when(info[2] == 0)
    def _():
        done[...] = near[...]

    @pl.when(info[1] == 1)
    def _():
        units, states = [], []
        for chunk in range(4):
            rows = slice(chunk * CHUNK, (chunk + 1) * CHUNK)
            for h in range(HEADS):
                k, v = head(h), head(HEADS + h)
                units.append((q[rows, k] if chunk < 3 else qd[:, k], [(done[:, k], done[:, v], None)]))
                states.append((state[h : h + 1, rows], state[HEADS + h : HEADS + h + 1, rows], mix[k, rows]))
        results = [(total, part) for _, total, part in pieces(units, states)]
        for chunk in range(4):
            finish(chunk, results[chunk * HEADS : (chunk + 1) * HEADS])

    @pl.when(info[1] == 0)
    def _():
        for chunk in range(4):
            rows = slice(chunk * CHUNK, (chunk + 1) * CHUNK)
            finish(chunk, [(state[HEADS + h : HEADS + h + 1, rows], mix[head(h), rows]) for h in range(HEADS)])

    for chunk in range(4):
        rows = pl.ds(pl.multiple_of((info[0] ^ chunk) * CHUNK, CHUNK), CHUNK)
        pltpu.make_async_copy(held.at[chunk], out.at[rows], sems.at[chunk]).wait()


EARLY = 20_000_000_000
FAR = 4_000_000_000
GATE = 1_000_000_000
GATE0 = 1_000_000_000
TP = 4


def device(ctx, tp):
    return ctx * TP + tp


def line_ends(ctx_count):
    return [(i, (i + ctx_count - 1) % ctx_count) for i in range(0, ctx_count, ROW)]


def body(series, w_query, w_key, w_value, block_pos):
    ctx_count = lax.axis_size("ctx")
    here = lax.axis_index("ctx")
    tp = lax.axis_index("tp")
    before = (here + ctx_count - 1) % ctx_count
    visible = block_pos[before] < block_pos[here]
    far_here = here % ROW == 0
    info = jnp.stack([tp, visible.astype(jnp.int32), far_here.astype(jnp.int32)]).astype(jnp.int32)
    weights = (w_query, w_key, w_value)
    ends = line_ends(ctx_count)

    def send(name, x, route):
        with jax.named_scope("n_" + name):
            return lax.ppermute(x, ("ctx", "tp"), route)

    def swap(name, x, pairs):
        return send(name, x, [(device(i, a), device(i, b)) for i in range(ctx_count) for a, b in pairs])

    def to_next(name, x):
        return send(name, x, [(device(i - 1, t), device(i, t)) for i in range(ctx_count) if i % ROW for t in range(TP)])

    def place(last, first, line):
        return first // (2 * ROW) * (2 * ROW) + last % (2 * ROW) - LAST + line

    def aside(name, x, places):
        return send(name, x, [(device(last, t), device(place(last, i, places[t]), t)) for i, last in ends for t in range(TP)])

    def across(name, x, chunk, places=None):
        route = []
        for i, last in ends:
            for t in range(TP):
                shard = t ^ chunk
                source = last if places is None else place(last, i, places[shard])
                route.append((device(source, shard), device(i, t)))
        return send(name, x, route)

    xc = swap("xc", series, [(t, t ^ 2) for t in range(TP)])
    xb = swap("xb", series, [(t, t ^ 1) for t in range(TP)])
    qa, kva = run(
        "own",
        project_own_body,
        (shape(CHUNK, WIDTH), shape(CHUNK, 2 * WIDTH)),
        [SMEM] + [VMEM] * 4,
        0,
        info,
        series,
        *weights,
    )
    far_c = across("across2", series, 2)
    far_b, far_d = (
        across(f"across{chunk}", aside(f"aside{chunk}", series, LEAVE[chunk]), chunk, LEAVE[chunk]) for chunk in (1, 3)
    )
    kva, far_c = lax.optimization_barrier((kva, far_c))
    far_a = across("across0", aside("aside0", kva, LEAVE[0]), 0, LEAVE[0])
    passed = run("gate0", gate_body, shape(8, 128, F32), [ANY], GATE0, xc)
    xc, own, qa, kva, passed = lax.optimization_barrier((xc, series, qa, kva, passed))
    outer = swap("outer", xc, [(2, 3), (1, 0)])
    passed = run("gate1", gate_body, shape(8, 128, F32), [ANY] * 2, GATE0, passed, far_c)
    own, far_c, passed = lax.optimization_barrier((own, far_c, passed))
    inner = swap("inner", own, [(1, 2), (2, 1)])
    q, kv = run(
        "middle",
        project_middle_body,
        (shape(HEAD, WIDTH), shape(HEAD, 2 * WIDTH)),
        [VMEM] * 7,
        0,
        xb,
        xc,
        qa,
        kva,
        *weights,
    )
    kv, far_d = lax.optimization_barrier((kv, far_d))
    near = to_next("near", kv)
    state, mix = run(
        "attend_own",
        own_first_body, STATE, [SMEM] + [VMEM] * 2, 0, info, q, kv)
    mix, far_b, far_c, far_d = lax.optimization_barrier((mix, far_b, far_c, far_d))
    far, far_last = run(
        "far",
        project_far_body,
        (shape(2 * CHUNK, 2 * WIDTH), shape(CHUNK, 2 * WIDTH)),
        [SMEM] + [ANY] * 5,
        FAR,
        info,
        far_b,
        far_c,
        far_d,
        w_key,
        w_value,
        scratch=(
            pltpu.VMEM((3, CHUNK, DEPTH), BF16),
            pltpu.VMEM((2, DEPTH, WIDTH), BF16),
            pltpu.SemaphoreType.DMA((5,)),
        ),
    )
    outer, far = lax.optimization_barrier((outer, far))
    passed = run("gate", gate_body, shape(8, 128, F32), [ANY] * 2, GATE, outer, passed)
    inner, passed = lax.optimization_barrier((inner, passed))
    kvd = run(
        "last",
        project_last_body,
        shape(CHUNK, 2 * WIDTH),
        [SMEM, ANY] + [VMEM] * 4,
        0,
        info,
        passed,
        outer,
        inner,
        w_key,
        w_value,
    )
    near_last = to_next("near_last", kvd)
    passed = run("gate2", gate_body, shape(8, 128, F32), [ANY] * 2, EARLY, kvd, far_a)
    near, kvd, outer, inner, passed = lax.optimization_barrier((near, kvd, outer, inner, passed))
    state, mix, qd = run(
        "attend_most",
        middle_body,
        (*STATE, shape(CHUNK, WIDTH)),
        [SMEM, ANY] + [VMEM] * 11,
        0,
        info,
        passed,
        outer,
        inner,
        w_query,
        q,
        kv,
        kvd,
        near,
        far_a,
        far,
        state,
        mix,
        alias={11: 0, 12: 1},
        scratch=(pltpu.VMEM((HEAD, 2 * WIDTH), BF16),),
    )
    return run(
        "attend_last",
        last_body,
        shape(BLOCK, WIDTH),
        [SMEM] + [VMEM] * 3 + [ANY] + [VMEM] * 2,
        0,
        info,
        q,
        qd,
        near_last,
        far_last,
        state,
        mix,
        out_specs=ANY,
        scratch=(
            pltpu.VMEM((4, CHUNK, WIDTH), BF16),
            pltpu.VMEM((CHUNK, 2 * WIDTH), BF16),
            pltpu.SemaphoreType.DMA((5,)),
        ),
    )


def solution(mesh):
    in_specs = (P(("ctx", "tp"), None), P(None, "tp"), P(None, "tp"), P(None, "tp"), P())
    out_specs = P("ctx", "tp")
    return jax.shard_map(body, mesh=mesh, in_specs=in_specs, out_specs=out_specs, check_vma=False)
```
